256 devices in a mesh: seq: 32 (over y_hi, z, core), chan: 8 (over y_lo, x).
Axes of the slice: x: 4, y: 4 (y_hi: 2, y_lo: 2; y = y_hi * 2 + y_lo), z: 8, core: 2. Of those that a mesh axis runs over, the one named last changes fastest.
Arguments:
- stream_in: bfloat16 [8192, 4096], P('seq'), may hold values from -6 to 6
- mr_proj: bfloat16 [8192, 3, 4096], P('seq', None, 'chan'), may hold values from -6 to 6
- mr_short: float32 [3, 3, 4096], P(None, None, 'chan'), may hold values from -3 to 3
- mr_filter: float32 [256, 128], P('chan'), may hold values from -0.5 to 0.5
- mr_out: bfloat16 [4096, 4096], P('chan', 'seq'), may hold values from -0.09375 to 0.09375
- li_gain: float32 [4096], replicated, may hold values from 0.5 to 1.5
- li_in: bfloat16 [4096, 3, 4096], P('seq', None, 'chan'), may hold values from -0.09375 to 0.09375
- li_short: float32 [3, 3, 4096], P(None, None, 'chan'), may hold values from -3 to 3
- li_res: float32 [16, 4096], P(None, 'chan'), may hold values from -0.09 to 0.09
- li_rate: float32 [16, 4096], P(None, 'chan'), may hold values from 6.1035156e-05 to 0.05
- li_skip: float32 [4096], P('chan'), may hold values from -4 to 4
Outputs:
- stream_out: bfloat16 [8192, 4096], P('seq', 'chan')
- li_output: bfloat16 [4096, 8192], P('chan', 'seq')
The draws below stay inside these ranges and needn't reach their ends.
All inputs are finite; a program needn't handle non-finite values.
Results may differ from the reference program's by a relative error of at most 0.04.
Values may be sent and summed in bfloat16 or wider, within the bound.
No kernel may reach another device: no remote copies, remote signals or barrier semaphores. Data moves between devices by JAX's collectives and lax.ppermute only.
A program may use at most 128 MiB of HBM per device.

```python
import math
import jax
import jax.numpy as jnp
from jax import lax

D = 4096
KMR = 128
GROUP = 16
MODES = 16
SEQ_LEN = 8192
GROUPS = 256


def block_scale(own_key, dims, split, low, high):
    level, own = 1.0, jax.random.fold_in(own_key, 6)
    for axis_at, parts in split:
        draws = jnp.exp(jax.random.uniform(jax.random.fold_in(own, axis_at), (parts,), jnp.float32, low / len(split), high / len(split)))
        level = level * jnp.repeat(draws, dims[axis_at] // parts).reshape([-1 if axis == axis_at else 1 for axis in range(len(dims))])
    return level


def centred(key, shape, spread, limit, shards=(), kind=jnp.bfloat16):
    result = jax.random.normal(key, shape, jnp.float32) * spread
    if len(shards) > 0:
        result = block_scale(key, shape, shards, -0.22, 0.18) * result
    return jnp.clip(result, min=-limit, max=limit).astype(kind)


def setup_inputs(seed: int = 0) -> dict:
    key_list = jax.random.split(jax.random.key(seed), 12)
    stream_in = centred(key_list[0], (SEQ_LEN, D), 1.0, 6.0, ((0, 32),))
    mr_proj = centred(key_list[1], (SEQ_LEN, 3, D), 1.0, 6.0, ((0, 32), (2, 8)))
    mr_short = centred(key_list[2], (3, 3, D), 0.6, 3.0, ((2, 8),), jnp.float32)
    mr_filter = centred(key_list[3], (GROUPS, KMR), KMR ** -0.5, 0.5, ((0, 8),), jnp.float32)
    mr_out = centred(key_list[4], (D, D), D ** -0.5, 0.09375, ((0, 8), (1, 32)))
    li_gain = jnp.clip(1.0 + 0.1 * jax.random.normal(key_list[5], (D,), jnp.float32), 0.5, 1.5)
    li_in = centred(key_list[6], (D, 3, D), D ** -0.5, 0.09375, ((0, 32), (2, 8)))
    li_short = centred(key_list[7], (3, 3, D), 0.6, 3.0, ((2, 8),), jnp.float32)
    li_res = centred(key_list[8], (MODES, D), 0.015, 0.09, ((1, 8),), jnp.float32)
    li_rate = jnp.clip(jnp.exp(math.log(0.05) - 6.7083283 * jax.random.uniform(key_list[9], (MODES, D), jnp.float32) ** block_scale(key_list[9], (MODES, D), ((1, 8),), -0.2, 0.2)), 6.103515625e-05, 0.05)
    li_skip = centred(key_list[10], (D,), 1.0, 4.0, ((0, 8),), jnp.float32)
    return dict(stream_in=stream_in, mr_proj=mr_proj, mr_short=mr_short, mr_filter=mr_filter, mr_out=mr_out, li_gain=li_gain, li_in=li_in, li_short=li_short, li_res=li_res, li_rate=li_rate, li_skip=li_skip)


EPSILON = 1e-06
HIGHEST = lax.Precision.HIGHEST

def short_filter(raw_rows, weights):
    row_count = raw_rows.shape[0]
    padded = jnp.concatenate([jnp.zeros((2,) + raw_rows.shape[1:], raw_rows.dtype), raw_rows], axis=0)
    running = weights[:, 0][None] * padded[2:2 + row_count]
    for lag_index in (1, 2):
        running = running + weights[:, lag_index][None] * padded[2 - lag_index:2 - lag_index + row_count]
    return running

def grouped_filter(values, filters):
    per_channel = jnp.repeat(filters, GROUP, axis=0)
    row_count = values.shape[0]
    tap_count = filters.shape[1]
    padded = jnp.concatenate([jnp.zeros((tap_count - 1, values.shape[1]), values.dtype), values], axis=0)

    def one_tap(lag_index, running):
        window = lax.dynamic_slice_in_dim(padded, tap_count - 1 - lag_index, row_count, 0)
        column = lax.dynamic_index_in_dim(per_channel, lag_index, 1, keepdims=False)
        return running + column[None] * window
    return lax.fori_loop(0, tap_count, one_tap, jnp.zeros_like(values))

def modal_long_filter(values, residues, rates, skip_gain):
    seq_length, chan_count = values.shape
    block_width = min(128, chan_count)
    block_count = chan_count // block_width
    lag_steps = jnp.arange(seq_length, dtype=jnp.float32)
    fft_length = 2 * seq_length

    def one_block(pieces_in):
        section, residue_set, rate_set, gain_set = pieces_in
        kernel = jnp.einsum('br,brl->bl', residue_set, jnp.exp(-rate_set[:, :, None] * lag_steps), precision=HIGHEST)
        spectrum = jnp.fft.rfft(section, n=fft_length) * jnp.fft.rfft(kernel, n=fft_length)
        convolved = jnp.fft.irfft(spectrum, n=fft_length)[:, :seq_length]
        return convolved + gain_set[:, None] * section
    channel_major = values.T.reshape(block_count, block_width, seq_length)
    residue_blocks = residues.T.reshape(block_count, block_width, residues.shape[0])
    rate_blocks = rates.T.reshape(block_count, block_width, rates.shape[0])
    gain_blocks = skip_gain.reshape(block_count, block_width)
    outputs = lax.map(one_block, (channel_major, residue_blocks, rate_blocks, gain_blocks))
    return outputs.reshape(chan_count, seq_length)

def reference(stream_in, mr_proj, mr_short, mr_filter, mr_out, li_gain, li_in, li_short, li_res, li_rate, li_skip):
    mr_mixed = short_filter(mr_proj.astype(jnp.float32), mr_short.astype(jnp.float32))
    mr_values = mr_mixed[:, 1] * mr_mixed[:, 2]
    mr_filtered = grouped_filter(mr_values, mr_filter.astype(jnp.float32))
    mr_gated = (mr_mixed[:, 0] * mr_filtered).astype(jnp.bfloat16)
    branch = jnp.dot(mr_gated, mr_out, preferred_element_type=jnp.float32)
    stream_out = (stream_in.astype(jnp.float32) + branch).astype(jnp.bfloat16)
    stream_wide = stream_out.astype(jnp.float32)
    inverse_rms = lax.rsqrt(lax.optimization_barrier(jnp.mean(stream_wide * stream_wide, axis=1, keepdims=True)) + EPSILON)
    normed = (stream_wide * inverse_rms * li_gain.astype(jnp.float32)[None]).astype(jnp.bfloat16)
    width_d = normed.shape[1]
    li_proj = jnp.dot(normed, li_in.reshape(width_d, 3 * width_d), preferred_element_type=jnp.float32)
    li_proj = li_proj.reshape(-1, 3, width_d).astype(jnp.bfloat16)
    li_mixed = short_filter(li_proj.astype(jnp.float32), li_short.astype(jnp.float32))
    li_values = (li_mixed[:, 1] * li_mixed[:, 2]).astype(jnp.bfloat16)
    li_filtered = modal_long_filter(li_values.astype(jnp.float32), li_res.astype(jnp.float32), li_rate.astype(jnp.float32), li_skip.astype(jnp.float32))
    li_output = (li_mixed[:, 0].T * li_filtered).astype(jnp.bfloat16)
    return (stream_out, li_output)
```

```python
import functools

import jax
import jax.numpy as jnp
from jax import lax
from jax.experimental import pallas as pl
from jax.experimental.pallas import tpu as pltpu
from jax.sharding import Mesh
from jax.sharding import PartitionSpec as P

BF = jnp.bfloat16
F32 = jnp.float32
EPSILON = 1e-06
SEQ = ("yh", "z", "core")
CHIPS = ("yh", "z")
CHAN = ("yl", "xx")
GROUP = 16
MIB = 1024 * 1024


def call(body, outs, ins, scratch=(), smem=(), vmem=32, cost=None):
    specs = [
        pl.BlockSpec(memory_space=pltpu.SMEM if i in smem else pltpu.VMEM) for i in range(len(ins))
    ]
    return pl.pallas_call(
        body,
        out_shape=[jax.ShapeDtypeStruct(s, d) for s, d in outs],
        in_specs=specs,
        out_specs=[pl.BlockSpec(memory_space=pltpu.VMEM)] * len(outs),
        scratch_shapes=list(scratch),
        compiler_params=pltpu.CompilerParams(vmem_limit_bytes=vmem * MIB),
        cost_estimate=cost,
    )(*ins)


def shifted(block, axis, distance):
    n = lax.axis_size(axis)
    return lax.ppermute(block, axis, [(i - distance, i) for i in range(distance, n)])


def turned(block, axis, distance):
    n = lax.axis_size(axis)
    return lax.ppermute(block, axis, [(i, (i + distance) % n) for i in range(n)])


def ring(block, axis):
    n = lax.axis_size(axis)
    out = [None] * n
    out[0] = block
    up = down = block
    for i in range(1, n // 2 + 1):
        up = turned(up, axis, 1)
        out[n - i] = up
        if i < n - i:
            down = turned(down, axis, -1)
            out[i] = down
    return out


def short3(ext, w):
    return w[0:1] * ext + w[1:2] * pltpu.roll(ext, 1, 0) + w[2:3] * pltpu.roll(ext, 2, 0)


def mr_body(proj, halo, short, rows, gated, vals):
    t = proj.shape[1]
    k = jnp.concatenate([halo[0:144].astype(F32), proj[1].astype(F32)], axis=0)
    v = jnp.concatenate([halo[144:288].astype(F32), proj[2].astype(F32)], axis=0)
    km = short3(k, short[1])
    vm = short3(v, short[2])
    vals[...] = (km * vm)[16:].astype(BF)
    q = jnp.concatenate([halo[288:304].astype(F32), proj[0].astype(F32)], axis=0)
    qm = short3(q, short[0])[16:]
    lane_group = lax.broadcasted_iota(jnp.int32, (128, 128), 1) // GROUP
    for tile in range(proj.shape[2] // 128):
        cols = slice(tile * 128, tile * 128 + 128)
        window = jnp.concatenate(
            [vals[b * 128 : b * 128 + 256, cols] for b in range(t // 128)], axis=1
        )
        acc = [jnp.zeros((128, 128), F32) for _ in range(t // 128)]
        for g in range(8):
            row = rows[tile * 8 + g : tile * 8 + g + 1, :]
            band = pltpu.roll(
                jnp.broadcast_to(row, (128, 256)), 0, 1, stride=1, stride_axis=0
            ).astype(BF)
            got = jnp.dot(band, window, preferred_element_type=F32)
            for b in range(t // 128):
                acc[b] = jnp.where(lane_group == g, got[:, b * 128 : b * 128 + 128], acc[b])
        for b in range(t // 128):
            r = slice(b * 128, b * 128 + 128)
            gated[r, cols] = (qm[r, cols] * acc[b]).astype(BF)


def branch_body(*refs):
    g0, g1 = refs[:2]
    weights = refs[2:10]
    out, ws = refs[10:]
    for j in range(8):
        ws[:, j * 128 : j * 128 + 128] = weights[j][...]
    for half, g in enumerate((g0, g1)):
        got = jnp.dot(g[...], ws[...], preferred_element_type=F32)
        for j in range(8):
            out[j, half * 256 : half * 256 + 256, :] = got[:, j * 128 : j * 128 + 128].astype(BF)


def stream_body(dh, place, recv, stream, out):
    for dk in range(2):
        r = slice(dk * 256, dk * 256 + 256)
        total = stream[(place[0] ^ dh) * 2 + (place[1] ^ dk)].astype(F32)
        for j in range(8):
            total = total + recv[j, r, :].astype(F32)
        total = total.astype(BF)
        for j in range(8):
            out[j, r, :] = total


def proj_body(*refs):
    acts, gain = refs[:2]
    weights = refs[2:10]
    own, send, a_s, w_s = refs[10:]
    for j in range(8):
        for p in range(3):
            w_s[j * 128 : j * 128 + 128, p * 512 : p * 512 + 512] = weights[j][p]
    lane = lax.broadcasted_iota(jnp.int32, (256, 128), 1)
    for dk in range(2):
        squares = jnp.zeros((256, 128), F32)
        for j in range(8):
            a = acts[j, dk * 256 : dk * 256 + 256, :].astype(F32)
            squares = squares + a * a
            a_s[:, j * 128 : j * 128 + 128] = (a * gain[j : j + 1, :]).astype(BF)
        total = jnp.sum(squares, axis=1, keepdims=True)
        for p in range(3):
            cols = slice(p * 512, p * 512 + 512)
            got = jnp.dot(a_s[...], w_s[:, cols], preferred_element_type=F32)
            if dk == 0:
                own[:, cols] = got
            else:
                send[:, cols] = got.astype(BF)
        if dk == 0:
            own[:, 1536:] = jnp.where(lane == 0, total, 0.0)
        else:
            send[:, 1536:] = in_two(total, lane)


def in_two(total, lane):
    high = total.astype(BF).astype(F32)
    return jnp.where(lane == 0, high, jnp.where(lane == 1, total - high, 0.0)).astype(BF)


def relay_body(own, recv, out):
    lane = lax.broadcasted_iota(jnp.int32, (256, 128), 1)
    out[:, :1536] = (own[:, :1536] + recv[:, :1536].astype(F32)).astype(BF)
    total = jnp.sum(own[:, 1536:] + recv[:, 1536:].astype(F32), axis=1, keepdims=True)
    out[:, 1536:] = in_two(total, lane)


def normed_body(width, own, recv, far, out, tail):
    sums = own[:, 1536:] + recv[:, 1536:].astype(F32) + far[:, 1536:].astype(F32)
    scale = lax.rsqrt(jnp.sum(sums, axis=1, keepdims=True) / width + EPSILON)
    for p in range(3):
        c = slice(p * 512, p * 512 + 512)
        got = own[:, c] + recv[:, c].astype(F32) + far[:, c].astype(F32)
        got = (got * scale).astype(BF)
        out[p] = got
        tail[p * 16 : p * 16 + 16, :] = got[240:, :]


def states_body(li, halo, short, rate, gate, vals, state):
    mixed = []
    for p in range(3):
        ext = jnp.concatenate(
            [halo[p * 16 : p * 16 + 16].astype(F32), li[p].astype(F32)], axis=0
        )
        mixed.append(short3(ext, short[p])[16:])
    gate[...] = mixed[0]
    vals[...] = (mixed[1] * mixed[2]).astype(BF).astype(F32)
    decay = jnp.exp(-rate[...])

    def eight(i, s):
        v = vals[pl.ds(pl.multiple_of(i * 8, 8), 8), :]
        for r in range(8):
            s = decay * s + v[r : r + 1, :]
        return s

    state[...] = lax.fori_loop(0, 32, eight, jnp.zeros_like(decay))


def output_body(gate, vals, entering, res, rate, skip, out, ys):
    decay = jnp.exp(-rate[...])
    residues = res[...]

    def eight(i, s):
        rows = pl.ds(pl.multiple_of(i * 8, 8), 8)
        v = vals[rows, :]
        got = []
        for r in range(8):
            s = decay * s + v[r : r + 1, :]
            got.append(jnp.sum(residues * s, axis=0, keepdims=True))
        y = jnp.concatenate(got, axis=0) + skip[...] * v
        ys[rows, :] = gate[rows, :] * y
        return s

    lax.fori_loop(0, 32, eight, entering[...])
    out[...] = ys[...].T.astype(BF)


def pick_body(place, acts0, acts1, out):
    for t in range(4):
        near = (place[0] ^ (t // 2)) == 0
        r = pl.ds(pl.multiple_of((place[1] ^ (t % 2)) * 256, 256), 256)
        for q in range(2):
            j = place[2 + q]
            cols = slice(q * 128, q * 128 + 128)

            @pl.when(near)
            def _():
                out[t, :, cols] = acts0[j, r, :]

            @pl.when(jnp.logical_not(near))
            def _():
                out[t, :, cols] = acts1[j, r, :]


def place_body(place, recv, out):
    for k in range(2):
        for q in range(2):
            out[:, q * 256 + k * 128 : q * 256 + k * 128 + 128] = recv[
                place[0] * 2 + k, :, q * 128 : q * 128 + 128
            ]


def local(
    stream_in,
    mr_proj,
    mr_short,
    mr_filter,
    mr_out,
    li_gain,
    li_in,
    li_short,
    li_res,
    li_rate,
    li_skip,
):
    h, z, k = (lax.axis_index(a) for a in SEQ)
    l, x = (lax.axis_index(a) for a in CHAN)
    c = l * 4 + x
    width = stream_in.shape[1]
    place = jnp.stack([h, k]).astype(jnp.int32)

    proj = jnp.transpose(mr_proj, (1, 0, 2))
    halo = shifted(
        jnp.concatenate([proj[1, -144:], proj[2, -144:], proj[0, -16:]], axis=0), SEQ, 1
    )
    out_blocks = ring(mr_out, "z")
    taps = mr_filter.shape[1]
    rows = jnp.pad(mr_filter[:, ::-1], ((0, 0), (1, 255 - taps)))
    (g00,) = call(
        mr_body,
        [((256, 512), BF)],
        [proj, halo, mr_short, rows],
        scratch=[pltpu.VMEM((384, 512), BF)],
    )
    stream4 = lax.dynamic_index_in_dim(
        stream_in.reshape(256, 2, 8, 2, 128), (z + c) % 8, 2, keepdims=False
    )
    stream4 = jnp.transpose(stream4, (1, 2, 0, 3)).reshape(4, 256, 128)
    stream4 = lax.all_to_all(stream4, ("yh", "core"), 0, 0, tiled=True)

    g10 = turned(g00, "yh", 1)
    g01 = turned(g00, "core", 1)
    g11 = turned(g10, "core", 1)
    li_blocks = ring(jnp.transpose(li_in, (1, 0, 2)), "z")
    gain = jnp.roll(li_gain.reshape(2, 8, 2, 128)[h, :, k], -z, axis=0)

    acts, own, recv = [], [], []
    for dh, pair in enumerate(((g00, g01), (g10, g11))):
        (parts,) = call(
            branch_body,
            [((8, 512, 128), BF)],
            [*pair, *out_blocks],
            scratch=[pltpu.VMEM((512, 1024), BF)],
        )
        parts = lax.all_to_all(parts, CHAN, 0, 0, tiled=True)
        (stream,) = call(
            functools.partial(stream_body, dh),
            [((8, 512, 128), BF)],
            [place, parts, stream4],
            smem=(0,),
        )
        acts.append(lax.all_to_all(stream, CHAN, 0, 0, tiled=True))
    for dh in range(2):
        mine, send = call(
            proj_body,
            [((256, 1664), F32), ((256, 1664), BF)],
            [acts[dh], gain, *li_blocks],
            scratch=[pltpu.VMEM((256, 1024), BF), pltpu.VMEM((1024, 1536), BF)],
        )
        own.append(mine)
        recv.append(turned(send, "core", 1))
    (relay,) = call(relay_body, [((256, 1664), BF)], [own[1], recv[1]])
    far = turned(relay, "yh", 1)
    li, tail = call(
        functools.partial(normed_body, float(width)),
        [((3, 256, 512), BF), ((48, 512), BF)],
        [own[0], recv[0], far],
    )
    gate, vals, state = call(
        states_body,
        [((256, 512), F32), ((256, 512), F32), ((16, 512), F32)],
        [li, shifted(tail, SEQ, 1), li_short, li_rate],
    )

    span = li.shape[1]

    def decay(n):
        return jnp.exp(-li_rate * float(span * n))

    other = turned(state, "core", 1)
    first = jnp.where(k == 0, state, other)
    second = jnp.where(k == 0, other, state)
    chip = second + decay(1) * first
    before = [shifted(chip, CHIPS, d) for d in (1, 2, 3)]
    entering = before[0] + decay(2) * before[1] + decay(4) * before[2]
    window = chip + decay(2) * entering
    for n, d in enumerate((4, 8, 12)):
        entering = entering + decay(6 + 8 * n) * shifted(window, CHIPS, d)
    entering = jnp.where(k == 0, entering, first + decay(1) * entering)

    (li_output,) = call(
        output_body,
        [((512, 256), BF)],
        [gate, vals, entering, li_res, li_rate, li_skip.reshape(1, 512)],
        scratch=[pltpu.VMEM((256, 512), F32)],
    )

    wanted = jnp.stack([h, k, (2 * x - z) % 8, (2 * x + 1 - z) % 8]).astype(jnp.int32)
    (picked,) = call(
        pick_body, [((4, 256, 256), BF)], [wanted, acts[0], acts[1]], smem=(0,)
    )
    picked = lax.all_to_all(picked, ("yh", "core"), 0, 0, tiled=True)
    (stream_out,) = call(
        place_body,
        [((256, 512), BF)],
        [jnp.stack([l]).astype(jnp.int32), picked],
        smem=(0,),
    )
    return (stream_out, li_output)


def solution(mesh):
    split = Mesh(mesh.devices.reshape(2, 8, 2, 2, 4), ("yh", "z", "core", "yl", "xx"))
    placed = (
        P(SEQ, None),
        P(SEQ, None, CHAN),
        P(None, None, CHAN),
        P(CHAN, None),
        P(CHAN, SEQ),
        P(),
        P(SEQ, None, CHAN),
        P(None, None, CHAN),
        P(None, CHAN),
        P(None, CHAN),
        P(CHAN),
    )
    return jax.shard_map(
        local,
        mesh=split,
        in_specs=placed,
        out_specs=(P(SEQ, CHAN), P(CHAN, SEQ)),
        check_vma=False,
    )
```

```python
import functools

import jax
import jax.numpy as jnp
from jax import lax
from jax.experimental import pallas as pl
from jax.experimental.pallas import tpu as pltpu
from jax.sharding import Mesh
from jax.sharding import PartitionSpec as P

BF = jnp.bfloat16
F32 = jnp.float32
EPSILON = 1e-06
SEQ = ("yh", "z", "core")
CHIPS = ("yh", "z")
CHAN = ("yl", "xx")
GROUP = 16
MIB = 1024 * 1024


def call(body, outs, ins, scratch=(), smem=(), left=(), vmem=32, cost=None):
    specs = [
        pl.BlockSpec(memory_space=pltpu.SMEM if i in smem else pl.ANY if i in left else pltpu.VMEM)
        for i in range(len(ins))
    ]
    return pl.pallas_call(
        body,
        out_shape=[jax.ShapeDtypeStruct(s, d) for s, d in outs],
        in_specs=specs,
        out_specs=[pl.BlockSpec(memory_space=pltpu.VMEM)] * len(outs),
        scratch_shapes=list(scratch),
        compiler_params=pltpu.CompilerParams(vmem_limit_bytes=vmem * MIB),
        cost_estimate=cost,
    )(*ins)


def shifted(block, axis, distance):
    n = lax.axis_size(axis)
    return lax.ppermute(block, axis, [(i - distance, i) for i in range(distance, n)])


def turned(block, axis, distance):
    n = lax.axis_size(axis)
    return lax.ppermute(block, axis, [(i, (i + distance) % n) for i in range(n)])


def ring(block, axis):
    n = lax.axis_size(axis)
    out = [None] * n
    out[0] = block
    up = down = block
    for i in range(1, n // 2 + 1):
        up = turned(up, axis, 1)
        out[n - i] = up
        if i < n - i:
            down = turned(down, axis, -1)
            out[i] = down
    return out


def short3(ext, w):
    return w[0:1] * ext + w[1:2] * pltpu.roll(ext, 1, 0) + w[2:3] * pltpu.roll(ext, 2, 0)


def mr_body(proj, halo, short, rows, gated, vals):
    t = proj.shape[1]
    k = jnp.concatenate([halo[0:144].astype(F32), proj[1].astype(F32)], axis=0)
    v = jnp.concatenate([halo[144:288].astype(F32), proj[2].astype(F32)], axis=0)
    km = short3(k, short[1])
    vm = short3(v, short[2])
    vals[...] = (km * vm)[16:].astype(BF)
    q = jnp.concatenate([halo[288:304].astype(F32), proj[0].astype(F32)], axis=0)
    qm = short3(q, short[0])[16:]
    lane_group = lax.broadcasted_iota(jnp.int32, (128, 128), 1) // GROUP
    for tile in range(proj.shape[2] // 128):
        cols = slice(tile * 128, tile * 128 + 128)
        window = jnp.concatenate(
            [vals[b * 128 : b * 128 + 256, cols] for b in range(t // 128)], axis=1
        )
        acc = [jnp.zeros((128, 128), F32) for _ in range(t // 128)]
        for g in range(8):
            row = rows[tile * 8 + g : tile * 8 + g + 1, :]
            band = pltpu.roll(
                jnp.broadcast_to(row, (128, 256)), 0, 1, stride=1, stride_axis=0
            ).astype(BF)
            got = jnp.dot(band, window, preferred_element_type=F32)
            for b in range(t // 128):
                acc[b] = jnp.where(lane_group == g, got[:, b * 128 : b * 128 + 128], acc[b])
        for b in range(t // 128):
            r = slice(b * 128, b * 128 + 128)
            gated[r, cols] = (qm[r, cols] * acc[b]).astype(BF)


def branch_body(*refs):
    parts, weights = refs[:4], refs[4:12]
    out, ws = refs[12:]
    for j in range(8):
        ws[:, j * 128 : j * 128 + 128] = weights[j][...]
    for n, g in enumerate(parts):
        got = jnp.dot(g[...], ws[...], preferred_element_type=F32)
        for j in range(8):
            out[j, n * 256 : n * 256 + 256, :] = got[:, j * 128 : j * 128 + 128].astype(BF)


def slice_body(place, stream, out):
    out[0] = stream[...]


def stream_body(dh, place, recv, stream, out):
    for dk in range(2):
        r = slice(dk * 256, dk * 256 + 256)
        total = stream[(place[0] ^ dh) * 2 + (place[1] ^ dk)].astype(F32)
        for j in range(8):
            total = total + recv[j, dh * 512 + dk * 256 : dh * 512 + dk * 256 + 256, :].astype(F32)
        total = total.astype(BF)
        for j in range(8):
            out[j, r, :] = total


def proj_body(*refs):
    place, acts, gain = refs[:3]
    weights = refs[3:11]
    own, send, a_s, w_s = refs[-4:]
    for j in range(8):
        for p in range(3):
            w_s[j * 128 : j * 128 + 128, p * 512 : p * 512 + 512] = weights[j][p]
    lane = lax.broadcasted_iota(jnp.int32, (256, 128), 1)
    for dk in (1, 0):
        squares = jnp.zeros((256, 128), F32)
        for j in range(8):
            a = acts[j, dk * 256 : dk * 256 + 256, :].astype(F32)
            squares = squares + a * a
            a_s[:, j * 128 : j * 128 + 128] = (a * gain[j : j + 1, :]).astype(BF)
        total = jnp.sum(squares, axis=1, keepdims=True)
        for p in range(3):
            cols = slice(p * 512, p * 512 + 512)
            got = jnp.dot(a_s[...], w_s[:, cols], preferred_element_type=F32)
            if dk == 0:
                own[:, cols] = got
            else:
                send[:, cols] = got.astype(BF)
        if dk == 0:
            own[:, 1536:] = jnp.where(lane == 0, total, 0.0)
        else:
            send[:, 1536:1664] = in_two(total, lane)
    for q in range(2):
        send[:, 1664 + q * 128 : 1792 + q * 128] = acts[place[2 + q], 256:, :]


def assemble(place, acts, recv, out, base):
    for q in range(2):
        mine = pl.multiple_of(base + q * 256 + place[1] * 128, 128)
        theirs = pl.multiple_of(base + q * 256 + 128 - place[1] * 128, 128)
        out[:, pl.ds(mine, 128)] = acts[place[2 + q], :256, :]
        out[:, pl.ds(theirs, 128)] = recv[:, 1664 + q * 128 : 1792 + q * 128]


def in_two(total, lane):
    high = total.astype(BF).astype(F32)
    return jnp.where(lane == 0, high, jnp.where(lane == 1, total - high, 0.0)).astype(BF)


def relay_body(place, own, recv, acts, out):
    lane = lax.broadcasted_iota(jnp.int32, (256, 128), 1)
    out[:, :1536] = (own[:, :1536] + recv[:, :1536].astype(F32)).astype(BF)
    total = jnp.sum(own[:, 1536:] + recv[:, 1536:1664].astype(F32), axis=1, keepdims=True)
    out[:, 1536:1664] = in_two(total, lane)
    assemble(place, acts, recv, out, 1664)


def normed_body(width, place, own, recv, far, acts, out, tail, stream):
    sums = own[:, 1536:] + recv[:, 1536:1664].astype(F32) + far[:, 1536:1664].astype(F32)
    scale = lax.rsqrt(jnp.sum(sums, axis=1, keepdims=True) / width + EPSILON)
    for p in range(3):
        c = slice(p * 512, p * 512 + 512)
        got = own[:, c] + recv[:, c].astype(F32) + far[:, c].astype(F32)
        got = (got * scale).astype(BF)
        out[p] = got
        tail[p * 16 : p * 16 + 16, :] = got[240:, :]

    @pl.when(place[0] == place[5])
    def _():
        assemble(place, acts, recv, stream, 0)

    @pl.when(place[0] != place[5])
    def _():
        stream[...] = far[:, 1664:]


def states_body(li, halo, short, rate, gate, vals, state):
    mixed = []
    for p in range(3):
        ext = jnp.concatenate(
            [halo[p * 16 : p * 16 + 16].astype(F32), li[p].astype(F32)], axis=0
        )
        mixed.append(short3(ext, short[p])[16:])
    gate[...] = mixed[0]
    vals[...] = (mixed[1] * mixed[2]).astype(BF).astype(F32)
    decay = jnp.exp(-rate[...])

    def eight(i, s):
        v = vals[pl.ds(pl.multiple_of(i * 8, 8), 8), :]
        for r in range(8):
            s = decay * s + v[r : r + 1, :]
        return s

    state[...] = lax.fori_loop(0, 32, eight, jnp.zeros_like(decay))


def chip_body(span, place, state, other, rate, out, first):
    low = place[1] == 0
    early = jnp.where(low, state[...], other[...])
    late = jnp.where(low, other[...], state[...])
    first[...] = early
    chip = (late + jnp.exp(-rate[...] * span) * early).astype(BF)
    for j in range(out.shape[0]):
        out[j] = chip


def output_body(span, place, gate, vals, chips, first, res, rate, skip, out, ys):
    rates = rate[...]
    decay = jnp.exp(-rates)
    over = jnp.exp(-rates * span)
    twice = jnp.exp(-rates * (2.0 * span))
    entering = jnp.zeros_like(rates)
    for j in range(chips.shape[0]):
        entering = jnp.where(j < place[4], twice * entering + chips[j].astype(F32), entering)
    entering = jnp.where(place[1] == 0, entering, first[...] + over * entering)
    residues = res[...]

    def eight(i, s):
        rows = pl.ds(pl.multiple_of(i * 8, 8), 8)
        v = vals[rows, :]
        got = []
        for r in range(8):
            s = decay * s + v[r : r + 1, :]
            got.append(jnp.sum(residues * s, axis=0, keepdims=True))
        y = jnp.concatenate(got, axis=0) + skip[...] * v
        ys[rows, :] = gate[rows, :] * y
        return s

    lax.fori_loop(0, 32, eight, entering)
    out[...] = ys[...].T.astype(BF)


def local(
    stream_in,
    mr_proj,
    mr_short,
    mr_filter,
    mr_out,
    li_gain,
    li_in,
    li_short,
    li_res,
    li_rate,
    li_skip,
):
    h, z, k = (lax.axis_index(a) for a in SEQ)
    l, x = (lax.axis_index(a) for a in CHAN)
    c = l * 4 + x
    width = stream_in.shape[1]
    place = jnp.stack([h, k, (2 * x - z) % 8, (2 * x + 1 - z) % 8, h * 8 + z, l]).astype(jnp.int32)

    proj = jnp.transpose(mr_proj, (1, 0, 2))
    halo = shifted(
        jnp.concatenate([proj[1, -144:], proj[2, -144:], proj[0, -16:]], axis=0), SEQ, 1
    )
    out_blocks = ring(mr_out, "z")
    taps = mr_filter.shape[1]
    rows = jnp.pad(mr_filter[:, ::-1], ((0, 0), (1, 255 - taps)))
    (g00,) = call(
        mr_body,
        [((256, 512), BF)],
        [proj, halo, mr_short, rows],
        scratch=[pltpu.VMEM((384, 512), BF)],
    )
    turn = jnp.reshape((z + c) % 8, (1,)).astype(jnp.int32)
    stream4 = pl.pallas_call(
        slice_body,
        out_shape=jax.ShapeDtypeStruct((4, 256, 128), BF),
        grid_spec=pltpu.PrefetchScalarGridSpec(
            num_scalar_prefetch=1,
            grid=(4,),
            in_specs=[
                pl.BlockSpec((256, 128), lambda t, turn: (0, (t // 2) * 16 + turn[0] * 2 + t % 2))
            ],
            out_specs=pl.BlockSpec((1, 256, 128), lambda t, turn: (t, 0, 0)),
        ),
    )(turn, stream_in)
    stream4 = lax.all_to_all(stream4, ("yh", "core"), 0, 0, tiled=True)

    g10 = turned(g00, "yh", 1)
    g01 = turned(g00, "core", 1)
    g11 = turned(g10, "core", 1)
    li_blocks = ring(jnp.transpose(li_in, (1, 0, 2)), "z")
    gain = jnp.roll(li_gain.reshape(2, 8, 2, 128)[h, :, k], -z, axis=0)

    (parts,) = call(
        branch_body,
        [((8, 1024, 128), BF)],
        [g00, g01, g10, g11, *out_blocks],
        scratch=[pltpu.VMEM((512, 1024), BF)],
    )
    parts = lax.all_to_all(parts, CHAN, 0, 0, tiled=True)

    def stream_of(dh):
        return call(
            functools.partial(stream_body, dh),
            [((8, 512, 128), BF)],
            [place, parts, stream4],
            smem=(0,),
        )[0]

    def product(acts, *after):
        mine, send = call(
            proj_body,
            [((256, 1664), F32), ((256, 1920), BF)],
            [place, acts, gain, *li_blocks, *after],
            scratch=[pltpu.VMEM((256, 1024), BF), pltpu.VMEM((1024, 1536), BF)],
            smem=(0,),
            left=(11,),
        )
        return mine, turned(send, "core", 1)

    stream1 = stream_of(1)
    acts1 = lax.all_to_all(stream1, CHAN, 0, 0, tiled=True)
    stream0, acts1 = lax.optimization_barrier((stream_of(0), acts1))
    acts0 = lax.all_to_all(stream0, CHAN, 0, 0, tiled=True)
    own1, recv1 = product(acts1)
    (relay,) = call(
        relay_body,
        [((256, 2176), BF)],
        [place, own1, recv1, acts1],
        smem=(0,),
    )
    far = turned(relay, "yh", 1)
    own0, recv0 = product(acts0, relay)
    li, tail, stream_out = call(
        functools.partial(normed_body, float(width)),
        [((3, 256, 512), BF), ((48, 512), BF), ((256, 512), BF)],
        [place, own0, recv0, far, acts0],
        smem=(0,),
    )
    gate, vals, state = call(
        states_body,
        [((256, 512), F32), ((256, 512), F32), ((16, 512), F32)],
        [li, shifted(tail, SEQ, 1), li_short, li_rate],
    )

    span = float(li.shape[1])
    chips, first = call(
        functools.partial(chip_body, span),
        [((16, 16, 512), BF), ((16, 512), F32)],
        [place, state, turned(state, "core", 1), li_rate],
        smem=(0,),
    )
    chips = lax.all_to_all(chips, CHIPS, 0, 0, tiled=True)
    (li_output,) = call(
        functools.partial(output_body, span),
        [((512, 256), BF)],
        [place, gate, vals, chips, first, li_res, li_rate, li_skip.reshape(1, 512)],
        scratch=[pltpu.VMEM((256, 512), F32)],
        smem=(0,),
    )
    return (stream_out, li_output)


def solution(mesh):
    split = Mesh(mesh.devices.reshape(2, 8, 2, 2, 4), ("yh", "z", "core", "yl", "xx"))
    placed = (
        P(SEQ, None),
        P(SEQ, None, CHAN),
        P(None, None, CHAN),
        P(CHAN, None),
        P(CHAN, SEQ),
        P(),
        P(SEQ, None, CHAN),
        P(None, None, CHAN),
        P(None, CHAN),
        P(None, CHAN),
        P(CHAN),
    )
    return jax.shard_map(
        local,
        mesh=split,
        in_specs=placed,
        out_specs=(P(SEQ, CHAN), P(CHAN, SEQ)),
        check_vma=False,
    )
```

```python
import functools

import jax
import jax.numpy as jnp
from jax import lax
from jax.experimental import pallas as pl
from jax.experimental.pallas import tpu as pltpu
from jax.sharding import Mesh
from jax.sharding import PartitionSpec as P

BF = jnp.bfloat16
F32 = jnp.float32
EPSILON = 1e-06
SEQ = ("yh", "z", "core")
CHIPS = ("yh", "z")
CHAN = ("yl", "xx")
GROUP = 16
MIB = 1024 * 1024


def call(body, outs, ins, scratch=(), smem=(), after=(), vmem=32, cost=None):
    given = len(ins)
    specs = [
        pl.BlockSpec(memory_space=pltpu.SMEM if i in smem else pltpu.VMEM) for i in range(given)
    ]
    specs = specs + [pl.BlockSpec(memory_space=pl.ANY)] * len(after)

    def kernel(*refs):
        body(*refs[:given], *refs[given + len(after) :])

    return pl.pallas_call(
        kernel,
        out_shape=[jax.ShapeDtypeStruct(s, d) for s, d in outs],
        in_specs=specs,
        out_specs=[pl.BlockSpec(memory_space=pltpu.VMEM)] * len(outs),
        scratch_shapes=list(scratch),
        compiler_params=pltpu.CompilerParams(vmem_limit_bytes=vmem * MIB),
        cost_estimate=cost,
    )(*ins, *after)


def shifted(block, axis, distance):
    n = lax.axis_size(axis)
    return lax.ppermute(block, axis, [(i - distance, i) for i in range(distance, n)])


def turned(block, axis, distance):
    n = lax.axis_size(axis)
    return lax.ppermute(block, axis, [(i, (i + distance) % n) for i in range(n)])


def ring(block, axis):
    n = lax.axis_size(axis)
    out = [None] * n
    out[0] = block
    up = down = block
    for i in range(1, n // 2 + 1):
        up = turned(up, axis, 1)
        out[n - i] = up
        if i < n - i:
            down = turned(down, axis, -1)
            out[i] = down
    return out


def short3(ext, w):
    return w[0:1] * ext + w[1:2] * pltpu.roll(ext, 1, 0) + w[2:3] * pltpu.roll(ext, 2, 0)


def mr_body(proj, halo, short, rows, gated, vals):
    t = proj.shape[1]
    k = jnp.concatenate([halo[0:144].astype(F32), proj[1].astype(F32)], axis=0)
    v = jnp.concatenate([halo[144:288].astype(F32), proj[2].astype(F32)], axis=0)
    km = short3(k, short[1])
    vm = short3(v, short[2])
    vals[...] = (km * vm)[16:].astype(BF)
    q = jnp.concatenate([halo[288:304].astype(F32), proj[0].astype(F32)], axis=0)
    qm = short3(q, short[0])[16:]
    lane_group = lax.broadcasted_iota(jnp.int32, (128, 128), 1) // GROUP
    for tile in range(proj.shape[2] // 128):
        cols = slice(tile * 128, tile * 128 + 128)
        window = jnp.concatenate(
            [vals[b * 128 : b * 128 + 256, cols] for b in range(t // 128)], axis=1
        )
        acc = [jnp.zeros((128, 128), F32) for _ in range(t // 128)]
        for g in range(8):
            row = rows[tile * 8 + g : tile * 8 + g + 1, :]
            band = pltpu.roll(
                jnp.broadcast_to(row, (128, 256)), 0, 1, stride=1, stride_axis=0
            ).astype(BF)
            got = jnp.dot(band, window, preferred_element_type=F32)
            for b in range(t // 128):
                acc[b] = jnp.where(lane_group == g, got[:, b * 128 : b * 128 + 128], acc[b])
        for b in range(t // 128):
            r = slice(b * 128, b * 128 + 128)
            gated[r, cols] = (qm[r, cols] * acc[b]).astype(BF)


def branch_body(*refs):
    parts, weights = refs[:4], refs[4:12]
    out, ws = refs[12:]
    for j in range(8):
        ws[:, j * 128 : j * 128 + 128] = weights[j][...]
    for n, g in enumerate(parts):
        got = jnp.dot(g[...], ws[...], preferred_element_type=F32)
        for j in range(8):
            out[j, n * 256 : n * 256 + 256, :] = got[:, j * 128 : j * 128 + 128].astype(BF)


def slice_body(place, stream, after, out):
    out[0] = stream[...]


def stream_body(recv, own, core, far, both, out):
    for n, rows in enumerate((own[0], core[...], far[0], both[...])):
        r = slice(n * 256, n * 256 + 256)
        total = rows.astype(F32)
        for j in range(8):
            total = total + recv[j, r, :].astype(F32)
        total = total.astype(BF)
        for j in range(8):
            out[j, r, :] = total


def proj_body(dh, *refs):
    place, acts, gain = refs[:3]
    weights = refs[3:11]
    own, send, rest, a_s, w_s = refs[11:]
    for j in range(8):
        for p in range(3):
            w_s[j * 128 : j * 128 + 128, p * 512 : p * 512 + 512] = weights[j][p]
    lane = lax.broadcasted_iota(jnp.int32, (256, 128), 1)
    for dk in (1, 0):
        squares = jnp.zeros((256, 128), F32)
        for j in range(8):
            a = acts[j, dh * 512 + dk * 256 : dh * 512 + dk * 256 + 256, :].astype(F32)
            squares = squares + a * a
            a_s[:, j * 128 : j * 128 + 128] = (a * gain[j : j + 1, :]).astype(BF)
        total = jnp.sum(squares, axis=1, keepdims=True)
        for p in range(3):
            cols = slice(p * 512, p * 512 + 512)
            got = jnp.dot(a_s[...], w_s[:, cols], preferred_element_type=F32)
            if dk == 0:
                own[:, cols] = got
            else:
                if p < 2:
                    send[:, cols] = got.astype(BF)
                else:
                    rest[:, :512] = got.astype(BF)
        if dk == 0:
            own[:, 1536:] = jnp.where(lane == 0, total, 0.0)
        else:
            rest[:, 512:640] = in_two(total, lane)
    for q in range(2):
        rest[:, 640 + q * 128 : 768 + q * 128] = acts[place[2 + q], dh * 512 + 256 : dh * 512 + 512, :]


def assemble(place, acts, rest, out, dh):
    for q in range(2):
        mine = pl.multiple_of(q * 256 + place[1] * 128, 128)
        theirs = pl.multiple_of(q * 256 + 128 - place[1] * 128, 128)
        out[:, pl.ds(mine, 128)] = acts[place[2 + q], dh * 512 : dh * 512 + 256, :]
        out[:, pl.ds(theirs, 128)] = rest[:, 640 + q * 128 : 768 + q * 128]


def in_two(total, lane):
    high = total.astype(BF).astype(F32)
    return jnp.where(lane == 0, high, jnp.where(lane == 1, total - high, 0.0)).astype(BF)


def relay_body(place, own, recv, rest, acts, out, stream):
    lane = lax.broadcasted_iota(jnp.int32, (256, 128), 1)
    out[:, :1024] = (own[:, :1024] + recv[...].astype(F32)).astype(BF)
    out[:, 1024:1536] = (own[:, 1024:1536] + rest[:, :512].astype(F32)).astype(BF)
    total = jnp.sum(own[:, 1536:] + rest[:, 512:640].astype(F32), axis=1, keepdims=True)
    out[:, 1536:] = in_two(total, lane)
    assemble(place, acts, rest, stream, 1)


def normed_body(width, place, own, recv, rest, far, acts, theirs, out, tail, stream):
    sums = own[:, 1536:] + rest[:, 512:640].astype(F32) + far[:, 1536:].astype(F32)
    scale = lax.rsqrt(jnp.sum(sums, axis=1, keepdims=True) / width + EPSILON)
    for p in range(3):
        c = slice(p * 512, p * 512 + 512)
        other = recv[:, c] if p < 2 else rest[:, :512]
        got = own[:, c] + other.astype(F32) + far[:, c].astype(F32)
        got = (got * scale).astype(BF)
        out[p] = got
        tail[p * 16 : p * 16 + 16, :] = got[240:, :]

    @pl.when(place[0] == place[5])
    def _():
        assemble(place, acts, rest, stream, 0)

    @pl.when(place[0] != place[5])
    def _():
        stream[...] = theirs[...]


def states_body(li, halo, short, rate, gate, vals, state):
    mixed = []
    for p in range(3):
        ext = jnp.concatenate(
            [halo[p * 16 : p * 16 + 16].astype(F32), li[p].astype(F32)], axis=0
        )
        mixed.append(short3(ext, short[p])[16:])
    gate[...] = mixed[0]
    vals[...] = (mixed[1] * mixed[2]).astype(BF).astype(F32)
    decay = jnp.exp(-rate[...])

    def eight(i, s):
        v = vals[pl.ds(pl.multiple_of(i * 8, 8), 8), :]
        for r in range(8):
            s = decay * s + v[r : r + 1, :]
        return s

    state[...] = lax.fori_loop(0, 32, eight, jnp.zeros_like(decay))


def chip_body(span, place, state, other, rate, out, first):
    low = place[1] == 0
    early = jnp.where(low, state[...], other[...])
    late = jnp.where(low, other[...], state[...])
    first[...] = early
    chip = (late + jnp.exp(-rate[...] * span) * early).astype(BF)
    for j in range(out.shape[0]):
        out[j] = chip


def output_body(span, place, gate, vals, chips, first, res, rate, skip, out, ys):
    rates = rate[...]
    decay = jnp.exp(-rates)
    over = jnp.exp(-rates * span)
    twice = jnp.exp(-rates * (2.0 * span))
    entering = jnp.zeros_like(rates)
    for j in range(chips.shape[0]):
        entering = jnp.where(j < place[4], twice * entering + chips[j].astype(F32), entering)
    entering = jnp.where(place[1] == 0, entering, first[...] + over * entering)
    residues = res[...]

    def eight(i, s):
        rows = pl.ds(pl.multiple_of(i * 8, 8), 8)
        v = vals[rows, :]
        got = []
        for r in range(8):
            s = decay * s + v[r : r + 1, :]
            got.append(jnp.sum(residues * s, axis=0, keepdims=True))
        y = jnp.concatenate(got, axis=0) + skip[...] * v
        ys[rows, :] = gate[rows, :] * y
        return s

    lax.fori_loop(0, 32, eight, entering)
    out[...] = ys[...].T.astype(BF)


def local(
    stream_in,
    mr_proj,
    mr_short,
    mr_filter,
    mr_out,
    li_gain,
    li_in,
    li_short,
    li_res,
    li_rate,
    li_skip,
):
    h, z, k = (lax.axis_index(a) for a in SEQ)
    l, x = (lax.axis_index(a) for a in CHAN)
    c = l * 4 + x
    width = stream_in.shape[1]
    place = jnp.stack([h, k, (2 * x - z) % 8, (2 * x + 1 - z) % 8, h * 8 + z, l]).astype(jnp.int32)

    proj = jnp.transpose(mr_proj, (1, 0, 2))
    halo = shifted(
        jnp.concatenate([proj[1, -144:], proj[2, -144:], proj[0, -16:]], axis=0), SEQ, 1
    )
    out_blocks = ring(mr_out, "z")
    taps = mr_filter.shape[1]
    rows = jnp.pad(mr_filter[:, ::-1], ((0, 0), (1, 255 - taps)))
    (g00,) = call(
        mr_body,
        [((256, 512), BF)],
        [proj, halo, mr_short, rows],
        scratch=[pltpu.VMEM((384, 512), BF)],
        after=[out_blocks[1], out_blocks[-1]],
    )
    g10 = turned(g00, "yh", 1)
    g01 = turned(g00, "core", 1)
    g11 = turned(g10, "core", 1)
    li_blocks = ring(jnp.transpose(li_in, (1, 0, 2)), "z")
    gain = jnp.roll(li_gain.reshape(2, 8, 2, 128)[h, :, k], -z, axis=0)

    (parts,) = call(
        branch_body,
        [((8, 1024, 128), BF)],
        [g00, g01, g10, g11, *out_blocks],
        scratch=[pltpu.VMEM((512, 1024), BF)],
    )
    turn = jnp.stack([(z + c) % 8, h, k]).astype(jnp.int32)
    residual = pl.pallas_call(
        slice_body,
        out_shape=jax.ShapeDtypeStruct((4, 256, 128), BF),
        grid_spec=pltpu.PrefetchScalarGridSpec(
            num_scalar_prefetch=1,
            grid=(4,),
            in_specs=[
                pl.BlockSpec(
                    (256, 128),
                    lambda n, t: (0, (t[1] ^ (n // 2)) * 16 + t[0] * 2 + (t[2] ^ (n % 2))),
                ),
                pl.BlockSpec(memory_space=pl.ANY),
            ],
            out_specs=pl.BlockSpec((1, 256, 128), lambda n, t: (n, 0, 0)),
        ),
    )(turn, stream_in, parts)
    residual_core = turned(residual[1], "core", 1)
    residual_far = turned(residual[2:], "yh", 1)
    residual_both = turned(residual_far[1], "core", 1)
    parts = lax.all_to_all(parts, CHAN, 0, 0, tiled=True)

    (stream,) = call(
        stream_body,
        [((8, 1024, 128), BF)],
        [parts, residual, residual_core, residual_far, residual_both],
        after=[li_blocks[n] for n in (1, 2, -1, -2)],
    )
    acts = lax.all_to_all(stream, CHAN, 0, 0, tiled=True)

    def product(dh, *after):
        mine, send, rest = call(
            functools.partial(proj_body, dh),
            [((256, 1664), F32), ((256, 1024), BF), ((256, 896), BF)],
            [place, acts, gain, *li_blocks],
            scratch=[pltpu.VMEM((256, 1024), BF), pltpu.VMEM((1024, 1536), BF)],
            smem=(0,),
            after=after,
        )
        return mine, turned(send, "core", 1), turned(rest, "core", 1)

    own1, recv1, rest1 = product(1)
    relay, theirs = call(
        relay_body,
        [((256, 1664), BF), ((256, 512), BF)],
        [place, own1, recv1, rest1, acts],
        smem=(0,),
    )
    far = turned(relay, "yh", 1)
    theirs = lax.ppermute(theirs, ("yh", "yl"), [(0, 2), (3, 1)])
    own0, recv0, rest0 = product(0, relay)
    li, tail, stream_out = call(
        functools.partial(normed_body, float(width)),
        [((3, 256, 512), BF), ((48, 512), BF), ((256, 512), BF)],
        [place, own0, recv0, rest0, far, acts, theirs],
        smem=(0,),
    )
    gate, vals, state = call(
        states_body,
        [((256, 512), F32), ((256, 512), F32), ((16, 512), F32)],
        [li, shifted(tail, SEQ, 1), li_short, li_rate],
    )

    span = float(li.shape[1])
    chips, first = call(
        functools.partial(chip_body, span),
        [((16, 16, 512), BF), ((16, 512), F32)],
        [place, state, turned(state, "core", 1), li_rate],
        smem=(0,),
    )
    chips = lax.all_to_all(chips, CHIPS, 0, 0, tiled=True)
    (li_output,) = call(
        functools.partial(output_body, span),
        [((512, 256), BF)],
        [place, gate, vals, chips, first, li_res, li_rate, li_skip.reshape(1, 512)],
        scratch=[pltpu.VMEM((256, 512), F32)],
        smem=(0,),
    )
    return (stream_out, li_output)


def solution(mesh):
    split = Mesh(mesh.devices.reshape(2, 8, 2, 2, 4), ("yh", "z", "core", "yl", "xx"))
    placed = (
        P(SEQ, None),
        P(SEQ, None, CHAN),
        P(None, None, CHAN),
        P(CHAN, None),
        P(CHAN, SEQ),
        P(),
        P(SEQ, None, CHAN),
        P(None, None, CHAN),
        P(None, CHAN),
        P(None, CHAN),
        P(CHAN),
    )
    return jax.shard_map(
        local,
        mesh=split,
        in_specs=placed,
        out_specs=(P(SEQ, CHAN), P(CHAN, SEQ)),
        check_vma=False,
    )
```

```python
import functools

import jax
import jax.numpy as jnp
from jax import lax
from jax.experimental import pallas as pl
from jax.experimental.pallas import tpu as pltpu
from jax.sharding import Mesh
from jax.sharding import PartitionSpec as P

BF = jnp.bfloat16
F32 = jnp.float32
EPSILON = 1e-06
SEQ = ("yh", "z", "core")
CHIPS = ("yh", "z")
CHAN = ("yl", "xx")
GROUP = 16
MIB = 1024 * 1024


def call(body, outs, ins, scratch=(), smem=(), after=(), vmem=32, cost=None):
    given = len(ins)
    specs = [
        pl.BlockSpec(memory_space=pltpu.SMEM if i in smem else pltpu.VMEM) for i in range(given)
    ]
    specs = specs + [pl.BlockSpec(memory_space=pl.ANY)] * len(after)

    def kernel(*refs):
        body(*refs[:given], *refs[given + len(after) :])

    return pl.pallas_call(
        kernel,
        out_shape=[jax.ShapeDtypeStruct(s, d) for s, d in outs],
        in_specs=specs,
        out_specs=[pl.BlockSpec(memory_space=pltpu.VMEM)] * len(outs),
        scratch_shapes=list(scratch),
        compiler_params=pltpu.CompilerParams(vmem_limit_bytes=vmem * MIB),
        cost_estimate=cost,
    )(*ins, *after)


def shifted(block, axis, distance):
    n = lax.axis_size(axis)
    return lax.ppermute(block, axis, [(i - distance, i) for i in range(distance, n)])


def turned(block, axis, distance):
    n = lax.axis_size(axis)
    return lax.ppermute(block, axis, [(i, (i + distance) % n) for i in range(n)])


def ring(block, axis):
    n = lax.axis_size(axis)
    out = [None] * n
    out[0] = block
    up = down = block
    for i in range(1, n // 2 + 1):
        up = turned(up, axis, 1)
        out[n - i] = up
        if i < n - i:
            down = turned(down, axis, -1)
            out[i] = down
    return out


def short3(ext, w):
    return w[0:1] * ext + w[1:2] * pltpu.roll(ext, 1, 0) + w[2:3] * pltpu.roll(ext, 2, 0)


def mr_body(proj, halo, short, rows, gated, vals):
    t = proj.shape[1]
    k = jnp.concatenate([halo[0:144].astype(F32), proj[1].astype(F32)], axis=0)
    v = jnp.concatenate([halo[144:288].astype(F32), proj[2].astype(F32)], axis=0)
    km = short3(k, short[1])
    vm = short3(v, short[2])
    vals[...] = (km * vm)[16:].astype(BF)
    q = jnp.concatenate([halo[288:304].astype(F32), proj[0].astype(F32)], axis=0)
    qm = short3(q, short[0])[16:]
    lane_group = lax.broadcasted_iota(jnp.int32, (128, 128), 1) // GROUP
    for tile in range(proj.shape[2] // 128):
        cols = slice(tile * 128, tile * 128 + 128)
        window = jnp.concatenate(
            [vals[b * 128 : b * 128 + 256, cols] for b in range(t // 128)], axis=1
        )
        acc = [jnp.zeros((128, 128), F32) for _ in range(t // 128)]
        for g in range(8):
            row = rows[tile * 8 + g : tile * 8 + g + 1, :]
            band = pltpu.roll(
                jnp.broadcast_to(row, (128, 256)), 0, 1, stride=1, stride_axis=0
            ).astype(BF)
            got = jnp.dot(band, window, preferred_element_type=F32)
            for b in range(t // 128):
                acc[b] = jnp.where(lane_group == g, got[:, b * 128 : b * 128 + 128], acc[b])
        for b in range(t // 128):
            r = slice(b * 128, b * 128 + 128)
            gated[r, cols] = (qm[r, cols] * acc[b]).astype(BF)


def branch_body(*refs):
    parts, weights = refs[:2], refs[2:10]
    out, ws = refs[10:]
    for j in range(8):
        for side in range(2):
            cols = slice(j * 256 + side * 128, j * 256 + side * 128 + 128)
            ws[:, cols] = weights[j][side * 512 : side * 512 + 512, :]
    for n, g in enumerate(parts):
        got = jnp.dot(g[...], ws[...], preferred_element_type=F32)
        for j in range(8):
            out[j, n * 256 : n * 256 + 256, :] = got[:, j * 256 : j * 256 + 256].astype(BF)


def slice_body(place, stream, after, out):
    out[0] = stream[...]


def stream_body(recv, own, core, out):
    for n, rows in enumerate((own[0], core[...])):
        r = slice(n * 256, n * 256 + 256)
        total = rows.astype(F32)
        for j in range(8):
            total = total + recv[j, r, :].astype(F32)
        total = total.astype(BF)
        for j in range(8):
            out[j, r, :] = total


def proj_body(*refs):
    place, acts, gain = refs[:3]
    near, away = refs[3:11], refs[11:19]
    own, send, rest, a_s, w_s = refs[19:]
    for j in range(8):
        for p in range(3):
            cols = slice(p * 512, p * 512 + 512)
            w_s[j * 256 : j * 256 + 128, cols] = near[j][p]
            w_s[j * 256 + 128 : j * 256 + 256, cols] = away[j][p]
    lane = lax.broadcasted_iota(jnp.int32, (256, 128), 1)
    for dk in (1, 0):
        squares = jnp.zeros((256, 256), F32)
        for j in range(8):
            a = acts[j, dk * 256 : dk * 256 + 256, :].astype(F32)
            squares = squares + a * a
            a_s[:, j * 256 : j * 256 + 256] = (a * gain[j : j + 1, :]).astype(BF)
        total = jnp.sum(squares, axis=1, keepdims=True)
        for p in range(3):
            cols = slice(p * 512, p * 512 + 512)
            got = jnp.dot(a_s[...], w_s[:, cols], preferred_element_type=F32)
            if dk == 0:
                own[:, cols] = got
            elif p < 2:
                send[:, cols] = got.astype(BF)
            else:
                rest[:, :512] = got.astype(BF)
        if dk == 0:
            own[:, 1536:] = jnp.where(lane == 0, total, 0.0)
        else:
            rest[:, 512:640] = in_two(total, lane)
    side = pl.multiple_of((place[0] ^ place[5]) * 128, 128)
    for q in range(2):
        rest[:, 640 + q * 128 : 768 + q * 128] = acts[place[2 + q], 256:, pl.ds(side, 128)]


def assemble(place, acts, rest, out):
    side = pl.multiple_of((place[0] ^ place[5]) * 128, 128)
    for q in range(2):
        mine = pl.multiple_of(q * 256 + place[1] * 128, 128)
        theirs = pl.multiple_of(q * 256 + 128 - place[1] * 128, 128)
        out[:, pl.ds(mine, 128)] = acts[place[2 + q], :256, pl.ds(side, 128)]
        out[:, pl.ds(theirs, 128)] = rest[:, 640 + q * 128 : 768 + q * 128]


def in_two(total, lane):
    high = total.astype(BF).astype(F32)
    return jnp.where(lane == 0, high, jnp.where(lane == 1, total - high, 0.0)).astype(BF)


def normed_body(width, place, own, recv, rest, acts, out, tail, stream):
    sums = own[:, 1536:] + rest[:, 512:640].astype(F32)
    scale = lax.rsqrt(jnp.sum(sums, axis=1, keepdims=True) / width + EPSILON)
    for p in range(3):
        c = slice(p * 512, p * 512 + 512)
        other = recv[:, c] if p < 2 else rest[:, :512]
        got = ((own[:, c] + other.astype(F32)) * scale).astype(BF)
        out[p] = got
        tail[p * 16 : p * 16 + 16, :] = got[240:, :]
    assemble(place, acts, rest, stream)


def states_body(li, halo, short, rate, gate, vals, state):
    mixed = []
    for p in range(3):
        ext = jnp.concatenate(
            [halo[p * 16 : p * 16 + 16].astype(F32), li[p].astype(F32)], axis=0
        )
        mixed.append(short3(ext, short[p])[16:])
    gate[...] = mixed[0]
    vals[...] = (mixed[1] * mixed[2]).astype(BF).astype(F32)
    decay = jnp.exp(-rate[...])

    def eight(i, s):
        v = vals[pl.ds(pl.multiple_of(i * 8, 8), 8), :]
        for r in range(8):
            s = decay * s + v[r : r + 1, :]
        return s

    state[...] = lax.fori_loop(0, 32, eight, jnp.zeros_like(decay))


def chip_body(span, place, state, other, rate, out, first):
    low = place[1] == 0
    early = jnp.where(low, state[...], other[...])
    late = jnp.where(low, other[...], state[...])
    first[...] = early
    chip = (late + jnp.exp(-rate[...] * span) * early).astype(BF)
    for j in range(out.shape[0]):
        out[j] = chip


def output_body(span, place, gate, vals, chips, first, res, rate, skip, out, ys):
    rates = rate[...]
    decay = jnp.exp(-rates)
    over = jnp.exp(-rates * span)
    twice = jnp.exp(-rates * (2.0 * span))
    entering = jnp.zeros_like(rates)
    for j in range(chips.shape[0]):
        entering = jnp.where(j < place[4], twice * entering + chips[j].astype(F32), entering)
    entering = jnp.where(place[1] == 0, entering, first[...] + over * entering)
    residues = res[...]

    def eight(i, s):
        rows = pl.ds(pl.multiple_of(i * 8, 8), 8)
        v = vals[rows, :]
        got = []
        for r in range(8):
            s = decay * s + v[r : r + 1, :]
            got.append(jnp.sum(residues * s, axis=0, keepdims=True))
        y = jnp.concatenate(got, axis=0) + skip[...] * v
        ys[rows, :] = gate[rows, :] * y
        return s

    lax.fori_loop(0, 32, eight, entering)
    out[...] = ys[...].T.astype(BF)


def local(
    stream_in,
    mr_proj,
    mr_short,
    mr_filter,
    mr_out,
    li_gain,
    li_in,
    li_short,
    li_res,
    li_rate,
    li_skip,
):
    h, z, k = (lax.axis_index(a) for a in SEQ)
    l, x = (lax.axis_index(a) for a in CHAN)
    c = l * 4 + x
    width = stream_in.shape[1]
    place = jnp.stack([h, k, (2 * x - z) % 8, (2 * x + 1 - z) % 8, h * 8 + z, l]).astype(jnp.int32)

    proj = jnp.transpose(mr_proj, (1, 0, 2))
    halo = shifted(
        jnp.concatenate([proj[1, -144:], proj[2, -144:], proj[0, -16:]], axis=0), SEQ, 1
    )
    out_blocks = ring(jnp.concatenate([mr_out, turned(mr_out, "yh", 1)], axis=0), "z")
    taps = mr_filter.shape[1]
    rows = jnp.pad(mr_filter[:, ::-1], ((0, 0), (1, 255 - taps)))
    (g00,) = call(
        mr_body,
        [((256, 512), BF)],
        [proj, halo, mr_short, rows],
        scratch=[pltpu.VMEM((384, 512), BF)],
        after=[out_blocks[1], out_blocks[-1]],
    )
    g01 = turned(g00, "core", 1)
    li_own = jnp.transpose(li_in, (1, 0, 2))
    li_side = turned(li_own, "yh", 1)
    li_near, li_away = ring(li_own, "z"), ring(li_side, "z")
    gain = jnp.roll(li_gain.reshape(2, 8, 2, 128)[:, :, k], (-h, -z), axis=(0, 1))
    gain = jnp.transpose(gain, (1, 0, 2)).reshape(8, 256)

    (parts,) = call(
        branch_body,
        [((8, 512, 256), BF)],
        [g00, g01, *out_blocks],
        scratch=[pltpu.VMEM((512, 2048), BF)],
        after=[li_side],
    )
    turn = jnp.stack([(z + c) % 8, h, k]).astype(jnp.int32)
    residual = pl.pallas_call(
        slice_body,
        out_shape=jax.ShapeDtypeStruct((2, 256, 256), BF),
        grid_spec=pltpu.PrefetchScalarGridSpec(
            num_scalar_prefetch=1,
            grid=(4,),
            in_specs=[
                pl.BlockSpec(
                    (256, 128),
                    lambda n, t: (0, (t[1] ^ (n % 2)) * 16 + t[0] * 2 + (t[2] ^ (n // 2))),
                ),
                pl.BlockSpec(memory_space=pl.ANY),
            ],
            out_specs=pl.BlockSpec((1, 256, 128), lambda n, t: (n // 2, 0, n % 2)),
        ),
    )(turn, stream_in, parts)
    residual_core = turned(residual[1], "core", 1)
    parts = lax.all_to_all(parts, CHAN, 0, 0, tiled=True)
    (stream,) = call(
        stream_body,
        [((8, 512, 256), BF)],
        [parts, residual, residual_core],
        after=[li_near[1], li_near[-1], li_away[1], li_away[-1], li_near[2], li_near[-2]],
    )
    acts = lax.all_to_all(stream, CHAN, 0, 0, tiled=True)
    own, send, rest = call(
        proj_body,
        [((256, 1664), F32), ((256, 1024), BF), ((256, 896), BF)],
        [place, acts, gain, *li_near, *li_away],
        scratch=[pltpu.VMEM((256, 2048), BF), pltpu.VMEM((2048, 1536), BF)],
        smem=(0,),
        vmem=26,
    )
    li, tail, stream_out = call(
        functools.partial(normed_body, float(width)),
        [((3, 256, 512), BF), ((48, 512), BF), ((256, 512), BF)],
        [place, own, turned(send, "core", 1), turned(rest, "core", 1), acts],
        smem=(0,),
    )
    gate, vals, state = call(
        states_body,
        [((256, 512), F32), ((256, 512), F32), ((16, 512), F32)],
        [li, shifted(tail, SEQ, 1), li_short, li_rate],
    )

    span = float(li.shape[1])
    chips, first = call(
        functools.partial(chip_body, span),
        [((16, 16, 512), BF), ((16, 512), F32)],
        [place, state, turned(state, "core", 1), li_rate],
        smem=(0,),
    )
    chips = lax.all_to_all(chips, CHIPS, 0, 0, tiled=True)
    (li_output,) = call(
        functools.partial(output_body, span),
        [((512, 256), BF)],
        [place, gate, vals, chips, first, li_res, li_rate, li_skip.reshape(1, 512)],
        scratch=[pltpu.VMEM((256, 512), F32)],
        smem=(0,),
    )
    return (stream_out, li_output)


def solution(mesh):
    split = Mesh(mesh.devices.reshape(2, 8, 2, 2, 4), ("yh", "z", "core", "yl", "xx"))
    placed = (
        P(SEQ, None),
        P(SEQ, None, CHAN),
        P(None, None, CHAN),
        P(CHAN, None),
        P(CHAN, SEQ),
        P(),
        P(SEQ, None, CHAN),
        P(None, None, CHAN),
        P(None, CHAN),
        P(None, CHAN),
        P(CHAN),
    )
    return jax.shard_map(
        local,
        mesh=split,
        in_specs=placed,
        out_specs=(P(SEQ, CHAN), P(CHAN, SEQ)),
        check_vma=False,
    )
```

```python
import functools

import jax
import jax.numpy as jnp
from jax import lax
from jax.experimental import pallas as pl
from jax.experimental.pallas import tpu as pltpu
from jax.sharding import Mesh
from jax.sharding import PartitionSpec as P

BF = jnp.bfloat16
F32 = jnp.float32
EPSILON = 1e-06
SEQ = ("yh", "z", "core")
CHIPS = ("yh", "z")
CHAN = ("yl", "xx")
GROUP = 16
MIB = 1024 * 1024


def call(body, outs, ins, scratch=(), smem=(), copied=(), after=(), vmem=32):
    given = len(ins)
    specs = [
        pl.BlockSpec(memory_space=pltpu.SMEM if i in smem else pl.ANY if i in copied else pltpu.VMEM)
        for i in range(given)
    ]
    specs = specs + [pl.BlockSpec(memory_space=pl.ANY)] * len(after)

    def kernel(*refs):
        body(*refs[:given], *refs[given + len(after) :])

    return pl.pallas_call(
        kernel,
        out_shape=[jax.ShapeDtypeStruct(s, d) for s, d in outs],
        in_specs=specs,
        out_specs=[pl.BlockSpec(memory_space=pltpu.VMEM)] * len(outs),
        scratch_shapes=list(scratch),
        compiler_params=pltpu.CompilerParams(vmem_limit_bytes=vmem * MIB),
    )(*ins, *after)


def shifted(block, axis, distance):
    n = lax.axis_size(axis)
    return lax.ppermute(block, axis, [(i - distance, i) for i in range(distance, n)])


def turned(block, axis, distance):
    n = lax.axis_size(axis)
    return lax.ppermute(block, axis, [(i, (i + distance) % n) for i in range(n)])


def ring(block, axis, way=1):
    n = lax.axis_size(axis)
    out = [None] * n
    out[0] = block
    up = down = block
    for i in range(1, n // 2 + 1):
        if i < n - i or way > 0:
            up = turned(up, axis, 1)
            out[n - i] = up
        if i < n - i or way < 0:
            down = turned(down, axis, -1)
            out[i] = down
    return out


def short3(ext, w):
    return w[0:1] * ext + w[1:2] * pltpu.roll(ext, 1, 0) + w[2:3] * pltpu.roll(ext, 2, 0)


def mr_body(proj, halo, short, rows, gated, vals):
    t = proj.shape[1]
    k = jnp.concatenate([halo[0:144].astype(F32), proj[1].astype(F32)], axis=0)
    v = jnp.concatenate([halo[144:288].astype(F32), proj[2].astype(F32)], axis=0)
    km = short3(k, short[1])
    vm = short3(v, short[2])
    vals[...] = (km * vm)[16:].astype(BF)
    q = jnp.concatenate([halo[288:304].astype(F32), proj[0].astype(F32)], axis=0)
    qm = short3(q, short[0])[16:]
    lane_group = lax.broadcasted_iota(jnp.int32, (128, 128), 1) // GROUP
    for tile in range(proj.shape[2] // 128):
        cols = slice(tile * 128, tile * 128 + 128)
        window = jnp.concatenate(
            [vals[b * 128 : b * 128 + 256, cols] for b in range(t // 128)], axis=1
        )
        acc = [jnp.zeros((128, 128), F32) for _ in range(t // 128)]
        for g in range(8):
            row = rows[tile * 8 + g : tile * 8 + g + 1, :]
            band = pltpu.roll(
                jnp.broadcast_to(row, (128, 256)), 0, 1, stride=1, stride_axis=0
            ).astype(BF)
            got = jnp.dot(band, window, preferred_element_type=F32)
            for b in range(t // 128):
                acc[b] = jnp.where(lane_group == g, got[:, b * 128 : b * 128 + 128], acc[b])
        for b in range(t // 128):
            r = slice(b * 128, b * 128 + 128)
            gated[r, cols] = (qm[r, cols] * acc[b]).astype(BF)


def branch_body(*refs):
    parts, weights = refs[:2], refs[2:10]
    out, ws = refs[10:]
    for j in range(8):
        for side in range(2):
            cols = slice(j * 256 + side * 128, j * 256 + side * 128 + 128)
            ws[:, cols] = weights[j][side * 512 : side * 512 + 512, :]
    for n, g in enumerate(parts):
        got = jnp.dot(g[...], ws[...], preferred_element_type=F32)
        for j in range(8):
            out[j, n * 256 : n * 256 + 256, :] = got[:, j * 256 : j * 256 + 256].astype(BF)


def slice_body(place, stream, after, out):
    out[...] = stream[...]


def stream_body(recv, own, core, after, *rest):
    out = rest[-1]
    total = jnp.where(pl.program_id(0) < 2, own[...], core[...]).astype(F32)
    for j in range(8):
        total = total + recv[j].astype(F32)
    total = total.astype(BF)
    for j in range(8):
        out[j] = total


ARRIVAL = (0, 1, 7, 2, 6, 3, 5, 4)


def scaled(acts, gain, rows, a_s):
    squares = jnp.zeros((256, 256), F32)
    for n, j in enumerate(ARRIVAL):
        a = acts[j, rows, :].astype(F32)
        squares = squares + a * a
        a_s[:, n * 256 : n * 256 + 256] = (a * gain[j : j + 1, :]).astype(BF)
    return jnp.sum(squares, axis=1, keepdims=True)


def weights_in(blocks, w_s, sems):
    copies = [
        pltpu.make_async_copy(block, w_s.at[:, n * 128 : n * 128 + 128, :], sems.at[n])
        for n, block in enumerate(blocks)
    ]
    for copy in copies:
        copy.start()
    return copies


def product(a_s, w_s, copies, p):
    depth = w_s.shape[1] // 2
    for half in range(2):
        rows = slice(half * depth, half * depth + depth)
        if p == 0:
            for copy in copies[half * 8 : half * 8 + 8]:
                copy.wait()
        got = jnp.dot(a_s[:, rows], w_s[p, rows, :], preferred_element_type=F32)
        total = got if half == 0 else total + got
    return total


def sent_body(*refs):
    place, acts, gain = refs[:3]
    send, rest, a_s, w_s, sems = refs[19:]
    copies = weights_in(refs[3:19], w_s, sems)
    lane = lax.broadcasted_iota(jnp.int32, (256, 128), 1)
    total = scaled(acts, gain, slice(256, 512), a_s)
    rest[:, 512:640] = in_two(total, lane)
    side = pl.multiple_of((place[0] ^ place[5]) * 128, 128)
    for q in range(2):
        rest[:, 640 + q * 128 : 768 + q * 128] = acts[place[2 + q], 256:, pl.ds(side, 128)]
    for p in range(3):
        got = product(a_s, w_s, copies, p).astype(BF)
        if p < 2:
            send[:, p * 512 : p * 512 + 512] = got
        else:
            rest[:, :512] = got


def kept_body(*refs):
    acts, gain = refs[:2]
    own, a_s, w_s, sems = refs[18:]
    copies = weights_in(refs[2:18], w_s, sems)
    lane = lax.broadcasted_iota(jnp.int32, (256, 128), 1)
    total = scaled(acts, gain, slice(0, 256), a_s)
    own[:, 1536:] = jnp.where(lane == 0, total, 0.0)
    for p in range(3):
        own[:, p * 512 : p * 512 + 512] = product(a_s, w_s, copies, p)


def assemble(place, acts, rest, out):
    side = pl.multiple_of((place[0] ^ place[5]) * 128, 128)
    for q in range(2):
        mine = pl.multiple_of(q * 256 + place[1] * 128, 128)
        theirs = pl.multiple_of(q * 256 + 128 - place[1] * 128, 128)
        out[:, pl.ds(mine, 128)] = acts[place[2 + q], :256, pl.ds(side, 128)]
        out[:, pl.ds(theirs, 128)] = rest[:, 640 + q * 128 : 768 + q * 128]


def in_two(total, lane):
    high = total.astype(BF).astype(F32)
    return jnp.where(lane == 0, high, jnp.where(lane == 1, total - high, 0.0)).astype(BF)


def normed_body(width, place, own, recv, rest, acts, out, tail, stream):
    sums = own[:, 1536:] + rest[:, 512:640].astype(F32)
    scale = lax.rsqrt(jnp.sum(sums, axis=1, keepdims=True) / width + EPSILON)
    for p in range(3):
        c = slice(p * 512, p * 512 + 512)
        other = recv[:, c] if p < 2 else rest[:, :512]
        got = ((own[:, c] + other.astype(F32)) * scale).astype(BF)
        out[p] = got
        tail[p * 16 : p * 16 + 16, :] = got[240:, :]
    assemble(place, acts, rest, stream)


def states_body(li, halo, short, rate, gate, vals, state):
    mixed = []
    for p in range(3):
        ext = jnp.concatenate(
            [halo[p * 16 : p * 16 + 16].astype(F32), li[p].astype(F32)], axis=0
        )
        mixed.append(short3(ext, short[p])[16:])
    gate[...] = mixed[0]
    vals[...] = (mixed[1] * mixed[2]).astype(BF).astype(F32)
    decay = jnp.exp(-rate[...])

    def eight(i, s):
        v = vals[pl.ds(pl.multiple_of(i * 8, 8), 8), :]
        for r in range(8):
            s = decay * s + v[r : r + 1, :]
        return s

    state[...] = lax.fori_loop(0, 32, eight, jnp.zeros_like(decay))


def chip_body(span, place, state, other, rate, out, first):
    low = place[1] == 0
    early = jnp.where(low, state[...], other[...])
    late = jnp.where(low, other[...], state[...])
    first[...] = early
    chip = (late + jnp.exp(-rate[...] * span) * early).astype(BF)
    for j in range(out.shape[0]):
        out[j] = chip


def echo_body(gate, vals, res, rate, skip, base):
    decay = jnp.exp(-rate[...])
    residues = res[...]

    def eight(i, s):
        rows = pl.ds(pl.multiple_of(i * 8, 8), 8)
        v = vals[rows, :]
        got = []
        for r in range(8):
            s = decay * s + v[r : r + 1, :]
            got.append(jnp.sum(residues * s, axis=0, keepdims=True))
        base[rows, :] = gate[rows, :] * (jnp.concatenate(got, axis=0) + skip[...] * v)
        return s

    lax.fori_loop(0, 32, eight, jnp.zeros_like(decay))


def output_body(span, place, chips, first, res, rate, gate, base, out, fade, ys):
    rates = rate[...]
    over = jnp.exp(-rates * span)
    twice = jnp.exp(-rates * (2.0 * span))
    entering = jnp.zeros_like(rates)
    for j in range(chips.shape[0]):
        entering = jnp.where(j < place[4], twice * entering + chips[j].astype(F32), entering)
    entering = jnp.where(place[1] == 0, entering, first[...] + over * entering)
    weights = res[...] * entering
    modes, tile = fade.shape[:2]
    step = (lax.broadcasted_iota(jnp.int32, fade.shape[1:], 0) + 1).astype(F32)
    for r in range(modes):
        fade[r] = jnp.exp(-rates[r : r + 1, :] * step)
    past = jnp.exp(-rates * float(tile))
    for b in range(ys.shape[0] // tile):
        rows = slice(b * tile, b * tile + tile)
        total = jnp.zeros(fade.shape[1:], F32)
        for r in range(modes):
            total = total + weights[r : r + 1, :] * fade[r]
        ys[rows, :] = base[rows, :] + gate[rows, :] * total
        weights = weights * past
    out[...] = ys[...].T.astype(BF)


def local(
    stream_in,
    mr_proj,
    mr_short,
    mr_filter,
    mr_out,
    li_gain,
    li_in,
    li_short,
    li_res,
    li_rate,
    li_skip,
):
    h, z, k = (lax.axis_index(a) for a in SEQ)
    l, x = (lax.axis_index(a) for a in CHAN)
    c = l * 4 + x
    width = stream_in.shape[1]
    place = jnp.stack([h, k, (2 * x - z) % 8, (2 * x + 1 - z) % 8, h * 8 + z, l]).astype(jnp.int32)

    proj = jnp.transpose(mr_proj, (1, 0, 2))
    halo = shifted(
        jnp.concatenate([proj[1, -144:], proj[2, -144:], proj[0, -16:]], axis=0), SEQ, 1
    )
    out_blocks = ring(jnp.concatenate([mr_out, turned(mr_out, "yh", 1)], axis=0), "z")
    taps = mr_filter.shape[1]
    rows = jnp.pad(mr_filter[:, ::-1], ((0, 0), (1, 255 - taps)))
    (g00,) = call(
        mr_body,
        [((256, 512), BF)],
        [proj, halo, mr_short, rows],
        scratch=[pltpu.VMEM((384, 512), BF)],
        after=[out_blocks[1], out_blocks[-1]],
    )
    g01 = turned(g00, "core", 1)
    li_own = jnp.transpose(li_in, (1, 0, 2))
    li_side = turned(li_own, "yh", 1)
    li_near, li_away = ring(li_own, "z"), ring(li_side, "z", -1)
    gain = jnp.roll(li_gain.reshape(2, 8, 2, 128)[:, :, k], (-h, -z), axis=(0, 1))
    gain = jnp.transpose(gain, (1, 0, 2)).reshape(8, 256)

    (parts,) = call(
        branch_body,
        [((8, 512, 256), BF)],
        [g00, g01, *out_blocks],
        scratch=[pltpu.VMEM((512, 2048), BF)],
        after=[li_side],
    )
    turn = jnp.stack([(z + c) % 8, h, k]).astype(jnp.int32)
    residual = []
    for dk in range(2):
        part = pl.pallas_call(
            slice_body,
            out_shape=jax.ShapeDtypeStruct((256, 256), BF),
            grid_spec=pltpu.PrefetchScalarGridSpec(
                num_scalar_prefetch=1,
                grid=(2,),
                in_specs=[
                    pl.BlockSpec(
                        (256, 128),
                        lambda n, t, dk=dk: (0, (t[1] ^ n) * 16 + t[0] * 2 + (t[2] ^ dk)),
                    ),
                    pl.BlockSpec(memory_space=pl.ANY),
                ],
                out_specs=pl.BlockSpec((256, 128), lambda n, t: (0, n)),
            ),
        )(turn, stream_in, parts)
        residual.append(part)
    residual[1] = turned(residual[1], "core", 1)
    parts = lax.all_to_all(parts, CHAN, 0, 0, tiled=True)
    before = [blocks[n] for blocks in (li_near, li_away) for n in (1, -1, 2, -2)]
    stream = pl.pallas_call(
        stream_body,
        out_shape=jax.ShapeDtypeStruct((8, 512, 256), BF),
        grid=(4,),
        in_specs=[
            pl.BlockSpec((8, 128, 256), lambda i: (0, i, 0)),
            pl.BlockSpec((128, 256), lambda i: (jnp.minimum(i, 1), 0)),
            pl.BlockSpec((128, 256), lambda i: (jnp.maximum(i - 2, 0), 0)),
            *[pl.BlockSpec(memory_space=pl.ANY)] * len(before),
        ],
        out_specs=pl.BlockSpec((8, 128, 256), lambda i: (0, i, 0)),
    )(parts, *residual, *before)
    acts = lax.all_to_all(stream, CHAN, 0, 0, tiled=True)
    weights = [blocks[j] for j in ARRIVAL for blocks in (li_near, li_away)]
    scratch = [
        pltpu.VMEM((256, 2048), BF),
        pltpu.VMEM((3, 2048, 512), BF),
        pltpu.SemaphoreType.DMA((16,)),
    ]
    send, rest = call(
        sent_body,
        [((256, 1024), BF), ((256, 896), BF)],
        [place, acts, gain, *weights],
        scratch=scratch,
        smem=(0,),
        copied=range(3, 19),
        vmem=58,
    )
    (own,) = call(
        kept_body,
        [((256, 1664), F32)],
        [acts, gain, *weights],
        scratch=scratch,
        copied=range(2, 18),
        vmem=58,
        after=[send],
    )
    li, tail, stream_out = call(
        functools.partial(normed_body, float(width)),
        [((3, 256, 512), BF), ((48, 512), BF), ((256, 512), BF)],
        [place, own, turned(send, "core", 1), turned(rest, "core", 1), acts],
        smem=(0,),
    )
    gate, vals, state = call(
        states_body,
        [((256, 512), F32), ((256, 512), F32), ((16, 512), F32)],
        [li, shifted(tail, SEQ, 1), li_short, li_rate],
    )

    span = float(li.shape[1])
    chips, first = call(
        functools.partial(chip_body, span),
        [((16, 16, 512), BF), ((16, 512), F32)],
        [place, state, turned(state, "core", 1), li_rate],
        smem=(0,),
    )
    chips = lax.all_to_all(chips, CHIPS, 0, 0, tiled=True)
    (base,) = call(
        echo_body,
        [((256, 512), F32)],
        [gate, vals, li_res, li_rate, li_skip.reshape(1, 512)],
        after=[first],
    )
    (li_output,) = call(
        functools.partial(output_body, span),
        [((512, 256), BF)],
        [place, chips, first, li_res, li_rate, gate, base],
        scratch=[pltpu.VMEM((16, 32, 512), F32), pltpu.VMEM((256, 512), F32)],
        smem=(0,),
    )
    return (stream_out, li_output)


def solution(mesh):
    split = Mesh(mesh.devices.reshape(2, 8, 2, 2, 4), ("yh", "z", "core", "yl", "xx"))
    placed = (
        P(SEQ, None),
        P(SEQ, None, CHAN),
        P(None, None, CHAN),
        P(CHAN, None),
        P(CHAN, SEQ),
        P(),
        P(SEQ, None, CHAN),
        P(None, None, CHAN),
        P(None, CHAN),
        P(None, CHAN),
        P(CHAN),
    )
    return jax.shard_map(
        local,
        mesh=split,
        in_specs=placed,
        out_specs=(P(SEQ, CHAN), P(CHAN, SEQ)),
        check_vma=False,
    )
```

```python
import functools

import jax
import jax.numpy as jnp
from jax import lax
from jax.experimental import pallas as pl
from jax.experimental.pallas import tpu as pltpu
from jax.sharding import Mesh
from jax.sharding import PartitionSpec as P

BF = jnp.bfloat16
F32 = jnp.float32
EPSILON = 1e-06
SEQ = ("yh", "z", "core")
CHIPS = ("yh", "z")
CHAN = ("yl", "xx")
GROUP = 16
MIB = 1024 * 1024


def call(body, outs, ins, scratch=(), smem=(), after=(), vmem=32):
    given = len(ins)
    specs = [
        pl.BlockSpec(memory_space=pltpu.SMEM if i in smem else pltpu.VMEM) for i in range(given)
    ]
    specs = specs + [pl.BlockSpec(memory_space=pl.ANY)] * len(after)

    def kernel(*refs):
        body(*refs[:given], *refs[given + len(after) :])

    return pl.pallas_call(
        kernel,
        out_shape=[jax.ShapeDtypeStruct(s, d) for s, d in outs],
        in_specs=specs,
        out_specs=[pl.BlockSpec(memory_space=pltpu.VMEM)] * len(outs),
        scratch_shapes=list(scratch),
        compiler_params=pltpu.CompilerParams(vmem_limit_bytes=vmem * MIB),
    )(*ins, *after)


def shifted(block, axis, distance):
    n = lax.axis_size(axis)
    return lax.ppermute(block, axis, [(i - distance, i) for i in range(distance, n)])


def turned(block, axis, distance):
    n = lax.axis_size(axis)
    return lax.ppermute(block, axis, [(i, (i + distance) % n) for i in range(n)])


def ring(block, axis, way=1):
    n = lax.axis_size(axis)
    out = [None] * n
    out[0] = block
    up = down = block
    for i in range(1, n // 2 + 1):
        if i < n - i or way > 0:
            up = turned(up, axis, 1)
            out[n - i] = up
        if i < n - i or way < 0:
            down = turned(down, axis, -1)
            out[i] = down
    return out


def short3(ext, w):
    return w[0:1] * ext + w[1:2] * pltpu.roll(ext, 1, 0) + w[2:3] * pltpu.roll(ext, 2, 0)


def mr_body(proj, halo, short, rows, gated, vals):
    t = proj.shape[1]
    k = jnp.concatenate([halo[0:144].astype(F32), proj[1].astype(F32)], axis=0)
    v = jnp.concatenate([halo[144:288].astype(F32), proj[2].astype(F32)], axis=0)
    km = short3(k, short[1])
    vm = short3(v, short[2])
    vals[...] = (km * vm)[16:].astype(BF)
    q = jnp.concatenate([halo[288:304].astype(F32), proj[0].astype(F32)], axis=0)
    qm = short3(q, short[0])[16:]
    lane_group = lax.broadcasted_iota(jnp.int32, (128, 128), 1) // GROUP
    for tile in range(proj.shape[2] // 128):
        cols = slice(tile * 128, tile * 128 + 128)
        window = jnp.concatenate(
            [vals[b * 128 : b * 128 + 256, cols] for b in range(t // 128)], axis=1
        )
        acc = [jnp.zeros((128, 128), F32) for _ in range(t // 128)]
        for g in range(8):
            row = rows[tile * 8 + g : tile * 8 + g + 1, :]
            band = pltpu.roll(
                jnp.broadcast_to(row, (128, 256)), 0, 1, stride=1, stride_axis=0
            ).astype(BF)
            got = jnp.dot(band, window, preferred_element_type=F32)
            for b in range(t // 128):
                acc[b] = jnp.where(lane_group == g, got[:, b * 128 : b * 128 + 128], acc[b])
        for b in range(t // 128):
            r = slice(b * 128, b * 128 + 128)
            gated[r, cols] = (qm[r, cols] * acc[b]).astype(BF)


def branch_body(*refs):
    parts, weights = refs[:2], refs[2:10]
    out, ws = refs[10:]
    for j in range(8):
        for side in range(2):
            cols = slice(j * 256 + side * 128, j * 256 + side * 128 + 128)
            ws[:, cols] = weights[j][side * 512 : side * 512 + 512, :]
    for n, g in enumerate(parts):
        got = jnp.dot(g[...], ws[...], preferred_element_type=F32)
        for j in range(8):
            out[j, n * 256 : n * 256 + 256, :] = got[:, j * 256 : j * 256 + 256].astype(BF)


def slice_body(place, stream, after, out):
    out[...] = stream[...]


def stream_body(recv, own, core, out):
    for n, rows in enumerate((own, core)):
        r = slice(n * 256, n * 256 + 256)
        total = rows[...].astype(F32)
        for j in range(8):
            total = total + recv[j, r, :].astype(F32)
        total = total.astype(BF)
        for j in range(8):
            out[j, r, :] = total


def proj_body(*refs):
    place, acts, gain = refs[:3]
    near, away = refs[3:11], refs[11:19]
    own, send, rest, a_s, w_s = refs[19:]
    for j in range(8):
        for p in range(3):
            cols = slice(p * 512, p * 512 + 512)
            w_s[j * 256 : j * 256 + 128, cols] = near[j][p]
            w_s[j * 256 + 128 : j * 256 + 256, cols] = away[j][p]
    lane = lax.broadcasted_iota(jnp.int32, (256, 128), 1)
    for dk in (1, 0):
        squares = jnp.zeros((256, 256), F32)
        for j in range(8):
            a = acts[j, dk * 256 : dk * 256 + 256, :].astype(F32)
            squares = squares + a * a
            a_s[:, j * 256 : j * 256 + 256] = (a * gain[j : j + 1, :]).astype(BF)
        total = jnp.sum(squares, axis=1, keepdims=True)
        for p in range(3):
            cols = slice(p * 512, p * 512 + 512)
            got = jnp.dot(a_s[...], w_s[:, cols], preferred_element_type=F32)
            if dk == 0:
                own[:, cols] = got
            elif p < 2:
                send[:, cols] = got.astype(BF)
            else:
                rest[:, :512] = got.astype(BF)
        if dk == 0:
            own[:, 1536:] = jnp.where(lane == 0, total, 0.0)
        else:
            rest[:, 512:640] = in_two(total, lane)
    side = pl.multiple_of((place[0] ^ place[5]) * 128, 128)
    for q in range(2):
        rest[:, 640 + q * 128 : 768 + q * 128] = acts[place[2 + q], 256:, pl.ds(side, 128)]


def assemble(place, acts, rest, out):
    side = pl.multiple_of((place[0] ^ place[5]) * 128, 128)
    for q in range(2):
        mine = pl.multiple_of(q * 256 + place[1] * 128, 128)
        theirs = pl.multiple_of(q * 256 + 128 - place[1] * 128, 128)
        out[:, pl.ds(mine, 128)] = acts[place[2 + q], :256, pl.ds(side, 128)]
        out[:, pl.ds(theirs, 128)] = rest[:, 640 + q * 128 : 768 + q * 128]


def in_two(total, lane):
    high = total.astype(BF).astype(F32)
    return jnp.where(lane == 0, high, jnp.where(lane == 1, total - high, 0.0)).astype(BF)


def normed_body(width, place, own, recv, rest, acts, out, tail, stream):
    sums = own[:, 1536:] + rest[:, 512:640].astype(F32)
    scale = lax.rsqrt(jnp.sum(sums, axis=1, keepdims=True) / width + EPSILON)
    for p in range(3):
        c = slice(p * 512, p * 512 + 512)
        other = recv[:, c] if p < 2 else rest[:, :512]
        got = ((own[:, c] + other.astype(F32)) * scale).astype(BF)
        out[p] = got
        tail[p * 16 : p * 16 + 16, :] = got[240:, :]
    assemble(place, acts, rest, stream)


def states_body(li, halo, short, rate, gate, vals, state):
    mixed = []
    for p in range(3):
        ext = jnp.concatenate(
            [halo[p * 16 : p * 16 + 16].astype(F32), li[p].astype(F32)], axis=0
        )
        mixed.append(short3(ext, short[p])[16:])
    gate[...] = mixed[0]
    vals[...] = (mixed[1] * mixed[2]).astype(BF).astype(F32)
    decay = jnp.exp(-rate[...])

    def eight(i, s):
        v = vals[pl.ds(pl.multiple_of(i * 8, 8), 8), :]
        for r in range(8):
            s = decay * s + v[r : r + 1, :]
        return s

    state[...] = lax.fori_loop(0, 32, eight, jnp.zeros_like(decay))


def chip_body(span, place, state, other, rate, out, first):
    low = place[1] == 0
    early = jnp.where(low, state[...], other[...])
    late = jnp.where(low, other[...], state[...])
    first[...] = early
    chip = (late + jnp.exp(-rate[...] * span) * early).astype(BF)
    for j in range(out.shape[0]):
        out[j] = chip


def echo_body(gate, vals, res, rate, skip, base):
    decay = jnp.exp(-rate[...])
    residues = res[...]

    def eight(i, s):
        rows = pl.ds(pl.multiple_of(i * 8, 8), 8)
        v = vals[rows, :]
        got = []
        for r in range(8):
            s = decay * s + v[r : r + 1, :]
            got.append(jnp.sum(residues * s, axis=0, keepdims=True))
        base[rows, :] = gate[rows, :] * (jnp.concatenate(got, axis=0) + skip[...] * v)
        return s

    lax.fori_loop(0, 32, eight, jnp.zeros_like(decay))


def output_body(span, place, chips, first, res, rate, gate, base, out, fade, ys):
    rates = rate[...]
    over = jnp.exp(-rates * span)
    twice = jnp.exp(-rates * (2.0 * span))
    entering = jnp.zeros_like(rates)
    for j in range(chips.shape[0]):
        entering = jnp.where(j < place[4], twice * entering + chips[j].astype(F32), entering)
    entering = jnp.where(place[1] == 0, entering, first[...] + over * entering)
    weights = res[...] * entering
    modes, tile = fade.shape[:2]
    step = (lax.broadcasted_iota(jnp.int32, fade.shape[1:], 0) + 1).astype(F32)
    for r in range(modes):
        fade[r] = jnp.exp(-rates[r : r + 1, :] * step)
    past = jnp.exp(-rates * float(tile))
    for b in range(ys.shape[0] // tile):
        rows = slice(b * tile, b * tile + tile)
        total = jnp.zeros(fade.shape[1:], F32)
        for r in range(modes):
            total = total + weights[r : r + 1, :] * fade[r]
        ys[rows, :] = base[rows, :] + gate[rows, :] * total
        weights = weights * past
    out[...] = ys[...].T.astype(BF)


def local(
    stream_in,
    mr_proj,
    mr_short,
    mr_filter,
    mr_out,
    li_gain,
    li_in,
    li_short,
    li_res,
    li_rate,
    li_skip,
):
    h, z, k = (lax.axis_index(a) for a in SEQ)
    l, x = (lax.axis_index(a) for a in CHAN)
    c = l * 4 + x
    width = stream_in.shape[1]
    place = jnp.stack([h, k, (2 * x - z) % 8, (2 * x + 1 - z) % 8, h * 8 + z, l]).astype(jnp.int32)

    proj = jnp.transpose(mr_proj, (1, 0, 2))
    halo = shifted(
        jnp.concatenate([proj[1, -144:], proj[2, -144:], proj[0, -16:]], axis=0), SEQ, 1
    )
    out_blocks = ring(jnp.concatenate([mr_out, turned(mr_out, "yh", 1)], axis=0), "z")
    taps = mr_filter.shape[1]
    rows = jnp.pad(mr_filter[:, ::-1], ((0, 0), (1, 255 - taps)))
    (g00,) = call(
        mr_body,
        [((256, 512), BF)],
        [proj, halo, mr_short, rows],
        scratch=[pltpu.VMEM((384, 512), BF)],
        after=[out_blocks[1], out_blocks[-1]],
    )
    g01 = turned(g00, "core", 1)
    li_own = jnp.transpose(li_in, (1, 0, 2))
    li_side = turned(li_own, "yh", 1)
    li_near, li_away = ring(li_own, "z"), ring(li_side, "z", -1)
    gain = jnp.roll(li_gain.reshape(2, 8, 2, 128)[:, :, k], (-h, -z), axis=(0, 1))
    gain = jnp.transpose(gain, (1, 0, 2)).reshape(8, 256)

    (parts,) = call(
        branch_body,
        [((8, 512, 256), BF)],
        [g00, g01, *out_blocks],
        scratch=[pltpu.VMEM((512, 2048), BF)],
        after=[li_side, li_near[1], li_near[-1]],
    )
    turn = jnp.stack([(z + c) % 8, h, k]).astype(jnp.int32)
    residual = []
    for dk in range(2):
        part = pl.pallas_call(
            slice_body,
            out_shape=jax.ShapeDtypeStruct((256, 256), BF),
            grid_spec=pltpu.PrefetchScalarGridSpec(
                num_scalar_prefetch=1,
                grid=(2,),
                in_specs=[
                    pl.BlockSpec(
                        (256, 128),
                        lambda n, t, dk=dk: (0, (t[1] ^ n) * 16 + t[0] * 2 + (t[2] ^ dk)),
                    ),
                    pl.BlockSpec(memory_space=pl.ANY),
                ],
                out_specs=pl.BlockSpec((256, 128), lambda n, t: (0, n)),
            ),
        )(turn, stream_in, parts)
        residual.append(part)
    residual[1] = turned(residual[1], "core", 1)
    parts = lax.all_to_all(parts, CHAN, 0, 0, tiled=True)
    (stream,) = call(
        stream_body,
        [((8, 512, 256), BF)],
        [parts, *residual],
        after=[blocks[n] for blocks in (li_near, li_away) for n in (1, -1, 2, -2)],
    )
    acts = lax.all_to_all(stream, CHAN, 0, 0, tiled=True)
    own, send, rest = call(
        proj_body,
        [((256, 1664), F32), ((256, 1024), BF), ((256, 896), BF)],
        [place, acts, gain, *li_near, *li_away],
        scratch=[pltpu.VMEM((256, 2048), BF), pltpu.VMEM((2048, 1536), BF)],
        smem=(0,),
        vmem=26,
    )
    li, tail, stream_out = call(
        functools.partial(normed_body, float(width)),
        [((3, 256, 512), BF), ((48, 512), BF), ((256, 512), BF)],
        [place, own, turned(send, "core", 1), turned(rest, "core", 1), acts],
        smem=(0,),
    )
    gate, vals, state = call(
        states_body,
        [((256, 512), F32), ((256, 512), F32), ((16, 512), F32)],
        [li, shifted(tail, SEQ, 1), li_short, li_rate],
    )

    span = float(li.shape[1])
    chips, first = call(
        functools.partial(chip_body, span),
        [((16, 16, 512), BF), ((16, 512), F32)],
        [place, state, turned(state, "core", 1), li_rate],
        smem=(0,),
    )
    chips = lax.all_to_all(chips, CHIPS, 0, 0, tiled=True)
    (base,) = call(
        echo_body,
        [((256, 512), F32)],
        [gate, vals, li_res, li_rate, li_skip.reshape(1, 512)],
        after=[first],
    )
    (li_output,) = call(
        functools.partial(output_body, span),
        [((512, 256), BF)],
        [place, chips, first, li_res, li_rate, gate, base],
        scratch=[pltpu.VMEM((16, 32, 512), F32), pltpu.VMEM((256, 512), F32)],
        smem=(0,),
    )
    return (stream_out, li_output)


def solution(mesh):
    split = Mesh(mesh.devices.reshape(2, 8, 2, 2, 4), ("yh", "z", "core", "yl", "xx"))
    placed = (
        P(SEQ, None),
        P(SEQ, None, CHAN),
        P(None, None, CHAN),
        P(CHAN, None),
        P(CHAN, SEQ),
        P(),
        P(SEQ, None, CHAN),
        P(None, None, CHAN),
        P(None, CHAN),
        P(None, CHAN),
        P(CHAN),
    )
    return jax.shard_map(
        local,
        mesh=split,
        in_specs=placed,
        out_specs=(P(SEQ, CHAN), P(CHAN, SEQ)),
        check_vma=False,
    )
```

```python
import functools

import jax
import jax.numpy as jnp
from jax import lax
from jax.experimental import pallas as pl
from jax.experimental.pallas import tpu as pltpu
from jax.sharding import Mesh
from jax.sharding import PartitionSpec as P

BF = jnp.bfloat16
F32 = jnp.float32
EPSILON = 1e-06
SEQ = ("yh", "z", "core")
CHIPS = ("yh", "z")
CHAN = ("yl", "xx")
GROUP = 16
MIB = 1024 * 1024


def call(body, outs, ins, scratch=(), smem=(), after=(), vmem=32):
    given = len(ins)
    specs = [
        pl.BlockSpec(memory_space=pltpu.SMEM if i in smem else pltpu.VMEM) for i in range(given)
    ]
    specs = specs + [pl.BlockSpec(memory_space=pl.ANY)] * len(after)

    def kernel(*refs):
        body(*refs[:given], *refs[given + len(after) :])

    return pl.pallas_call(
        kernel,
        out_shape=[jax.ShapeDtypeStruct(s, d) for s, d in outs],
        in_specs=specs,
        out_specs=[pl.BlockSpec(memory_space=pltpu.VMEM)] * len(outs),
        scratch_shapes=list(scratch),
        compiler_params=pltpu.CompilerParams(vmem_limit_bytes=vmem * MIB),
    )(*ins, *after)


def shifted(block, axis, distance):
    n = lax.axis_size(axis)
    return lax.ppermute(block, axis, [(i - distance, i) for i in range(distance, n)])


def turned(block, axis, distance):
    n = lax.axis_size(axis)
    return lax.ppermute(block, axis, [(i, (i + distance) % n) for i in range(n)])


def ring(block, axis, way=1):
    n = lax.axis_size(axis)
    out = [None] * n
    out[0] = block
    up = down = block
    for i in range(1, n // 2 + 1):
        if i < n - i or way > 0:
            up = turned(up, axis, 1)
            out[n - i] = up
        if i < n - i or way < 0:
            down = turned(down, axis, -1)
            out[i] = down
    return out


def short3(ext, w):
    return w[0:1] * ext + w[1:2] * pltpu.roll(ext, 1, 0) + w[2:3] * pltpu.roll(ext, 2, 0)


def mr_body(proj, halo, short, rows, gated, vals):
    t = proj.shape[1]
    k = jnp.concatenate([halo[0:144].astype(F32), proj[1].astype(F32)], axis=0)
    v = jnp.concatenate([halo[144:288].astype(F32), proj[2].astype(F32)], axis=0)
    km = short3(k, short[1])
    vm = short3(v, short[2])
    vals[...] = (km * vm)[16:].astype(BF)
    q = jnp.concatenate([halo[288:304].astype(F32), proj[0].astype(F32)], axis=0)
    qm = short3(q, short[0])[16:]
    lane_group = lax.broadcasted_iota(jnp.int32, (128, 128), 1) // GROUP
    for tile in range(proj.shape[2] // 128):
        cols = slice(tile * 128, tile * 128 + 128)
        window = jnp.concatenate(
            [vals[b * 128 : b * 128 + 256, cols] for b in range(t // 128)], axis=1
        )
        acc = [jnp.zeros((128, 128), F32) for _ in range(t // 128)]
        for g in range(8):
            row = rows[tile * 8 + g : tile * 8 + g + 1, :]
            band = pltpu.roll(
                jnp.broadcast_to(row, (128, 256)), 0, 1, stride=1, stride_axis=0
            ).astype(BF)
            got = jnp.dot(band, window, preferred_element_type=F32)
            for b in range(t // 128):
                acc[b] = jnp.where(lane_group == g, got[:, b * 128 : b * 128 + 128], acc[b])
        for b in range(t // 128):
            r = slice(b * 128, b * 128 + 128)
            gated[r, cols] = (qm[r, cols] * acc[b]).astype(BF)


def branch_body(*refs):
    parts, weights = refs[:4], refs[4:12]
    out, ws = refs[12:]
    for j in range(8):
        ws[:, j * 128 : j * 128 + 128] = weights[j][...]
    for n in range(2):
        got = jnp.dot(parts[n][...], ws[:512, :], preferred_element_type=F32)
        got = got + jnp.dot(parts[2 + n][...], ws[512:, :], preferred_element_type=F32)
        for j in range(4):
            out[j, n * 256 : n * 256 + 256, :] = got[:, j * 256 : j * 256 + 256].astype(BF)


def slice_body(place, stream, after, out):
    out[...] = stream[...]


def stream_body(recv, own, core, out):
    for n, rows in enumerate((own, core)):
        r = slice(n * 256, n * 256 + 256)
        total = rows[...].astype(F32)
        for j in range(recv.shape[0]):
            total = total + recv[j, r, :].astype(F32)
        total = total.astype(BF)
        for j in range(out.shape[0]):
            out[j, r, :] = total


def proj_body(*refs):
    place, acts, gain = refs[:3]
    near, away = refs[3:11], refs[11:19]
    own, send, rest, a_s, w_s = refs[19:]
    for j in range(8):
        for p in range(3):
            cols = slice(p * 512, p * 512 + 512)
            w_s[j * 256 : j * 256 + 128, cols] = near[j][p]
            w_s[j * 256 + 128 : j * 256 + 256, cols] = away[j][p]
    lane = lax.broadcasted_iota(jnp.int32, (256, 128), 1)
    for dk in (1, 0):
        squares = jnp.zeros((256, 128), F32)
        for j in range(8):
            for side in range(2):
                half = slice((j % 2) * 128, (j % 2) * 128 + 128)
                a = acts[
                    (place[0] ^ side) * 4 + j // 2, dk * 256 : dk * 256 + 256, half
                ].astype(F32)
                squares = squares + a * a
                scale = gain[j : j + 1, side * 128 : side * 128 + 128]
                cols = slice(j * 256 + side * 128, j * 256 + side * 128 + 128)
                a_s[:, cols] = (a * scale).astype(BF)
        total = jnp.sum(squares, axis=1, keepdims=True)
        for p in range(3):
            cols = slice(p * 512, p * 512 + 512)
            got = jnp.dot(a_s[...], w_s[:, cols], preferred_element_type=F32)
            if dk == 0:
                own[:, cols] = got
            elif p < 2:
                send[:, cols] = got.astype(BF)
            else:
                rest[:, :512] = got.astype(BF)
        if dk == 0:
            own[:, 1536:] = jnp.where(lane == 0, total, 0.0)
        else:
            rest[:, 512:640] = in_two(total, lane)
    for q in range(2):
        half = pl.multiple_of((place[2 + q] & 1) * 128, 128)
        block = place[5] * 4 + (place[2 + q] >> 1)
        rest[:, 640 + q * 128 : 768 + q * 128] = acts[block, 256:, pl.ds(half, 128)]


def assemble(place, acts, rest, out):
    for q in range(2):
        half = pl.multiple_of((place[2 + q] & 1) * 128, 128)
        block = place[5] * 4 + (place[2 + q] >> 1)
        mine = pl.multiple_of(q * 256 + place[1] * 128, 128)
        theirs = pl.multiple_of(q * 256 + 128 - place[1] * 128, 128)
        out[:, pl.ds(mine, 128)] = acts[block, :256, pl.ds(half, 128)]
        out[:, pl.ds(theirs, 128)] = rest[:, 640 + q * 128 : 768 + q * 128]


def in_two(total, lane):
    high = total.astype(BF).astype(F32)
    return jnp.where(lane == 0, high, jnp.where(lane == 1, total - high, 0.0)).astype(BF)


def normed_body(width, place, own, recv, rest, acts, out, tail, stream):
    sums = own[:, 1536:] + rest[:, 512:640].astype(F32)
    scale = lax.rsqrt(jnp.sum(sums, axis=1, keepdims=True) / width + EPSILON)
    for p in range(3):
        c = slice(p * 512, p * 512 + 512)
        other = recv[:, c] if p < 2 else rest[:, :512]
        got = ((own[:, c] + other.astype(F32)) * scale).astype(BF)
        out[p] = got
        tail[p * 16 : p * 16 + 16, :] = got[240:, :]
    assemble(place, acts, rest, stream)


def states_body(li, halo, short, rate, gate, vals, state):
    mixed = []
    for p in range(3):
        ext = jnp.concatenate(
            [halo[p * 16 : p * 16 + 16].astype(F32), li[p].astype(F32)], axis=0
        )
        mixed.append(short3(ext, short[p])[16:])
    gate[...] = mixed[0]
    vals[...] = (mixed[1] * mixed[2]).astype(BF).astype(F32)
    decay = jnp.exp(-rate[...])

    def eight(i, s):
        v = vals[pl.ds(pl.multiple_of(i * 8, 8), 8), :]
        for r in range(8):
            s = decay * s + v[r : r + 1, :]
        return s

    state[...] = lax.fori_loop(0, 32, eight, jnp.zeros_like(decay))


def chip_body(span, place, state, other, rate, out, first):
    low = place[1] == 0
    early = jnp.where(low, state[...], other[...])
    late = jnp.where(low, other[...], state[...])
    first[...] = early
    chip = (late + jnp.exp(-rate[...] * span) * early).astype(BF)
    for j in range(out.shape[0]):
        out[j] = chip


def echo_body(gate, vals, res, rate, skip, base):
    decay = jnp.exp(-rate[...])
    residues = res[...]

    def eight(i, s):
        rows = pl.ds(pl.multiple_of(i * 8, 8), 8)
        v = vals[rows, :]
        got = []
        for r in range(8):
            s = decay * s + v[r : r + 1, :]
            got.append(jnp.sum(residues * s, axis=0, keepdims=True))
        base[rows, :] = gate[rows, :] * (jnp.concatenate(got, axis=0) + skip[...] * v)
        return s

    lax.fori_loop(0, 32, eight, jnp.zeros_like(decay))


def output_body(span, place, chips, first, res, rate, gate, base, out, fade, ys):
    rates = rate[...]
    over = jnp.exp(-rates * span)
    twice = jnp.exp(-rates * (2.0 * span))
    entering = jnp.zeros_like(rates)
    for j in range(chips.shape[0]):
        entering = jnp.where(j < place[4], twice * entering + chips[j].astype(F32), entering)
    entering = jnp.where(place[1] == 0, entering, first[...] + over * entering)
    weights = res[...] * entering
    modes, tile = fade.shape[:2]
    step = (lax.broadcasted_iota(jnp.int32, fade.shape[1:], 0) + 1).astype(F32)
    for r in range(modes):
        fade[r] = jnp.exp(-rates[r : r + 1, :] * step)
    past = jnp.exp(-rates * float(tile))
    for b in range(ys.shape[0] // tile):
        rows = slice(b * tile, b * tile + tile)
        total = jnp.zeros(fade.shape[1:], F32)
        for r in range(modes):
            total = total + weights[r : r + 1, :] * fade[r]
        ys[rows, :] = base[rows, :] + gate[rows, :] * total
        weights = weights * past
    out[...] = ys[...].T.astype(BF)


def local(
    stream_in,
    mr_proj,
    mr_short,
    mr_filter,
    mr_out,
    li_gain,
    li_in,
    li_short,
    li_res,
    li_rate,
    li_skip,
):
    h, z, k = (lax.axis_index(a) for a in SEQ)
    l, x = (lax.axis_index(a) for a in CHAN)
    width = stream_in.shape[1]
    place = jnp.stack([h, k, (2 * x - z) % 8, (2 * x + 1 - z) % 8, h * 8 + z, l]).astype(jnp.int32)

    proj = jnp.transpose(mr_proj, (1, 0, 2))
    halo = shifted(
        jnp.concatenate([proj[1, -144:], proj[2, -144:], proj[0, -16:]], axis=0), SEQ, 1
    )
    here = mr_out
    first = lax.ppermute(here, ("yh", "yl"), [(1, 0), (2, 3), (0, 2), (3, 1)])
    second = lax.ppermute(here, ("yh", "yl"), [(1, 2), (2, 1)])
    pair = [jnp.where(h == l, here, first), jnp.where(h == l, first, second)]
    out_blocks = ring(jnp.concatenate(pair, axis=0), "z")
    taps = mr_filter.shape[1]
    rows = jnp.pad(mr_filter[:, ::-1], ((0, 0), (1, 255 - taps)))
    (g00,) = call(
        mr_body,
        [((256, 512), BF)],
        [proj, halo, mr_short, rows],
        scratch=[pltpu.VMEM((384, 512), BF)],
        after=[out_blocks[1], out_blocks[-1]],
    )
    across = turned(g00, "yl", 1)
    g01, across_core = turned(g00, "core", 1), turned(across, "core", 1)
    li_own = jnp.transpose(li_in, (1, 0, 2))
    li_side = turned(li_own, "yh", 1)
    li_near, li_away = ring(li_own, "z"), ring(li_side, "z", -1)
    gain = jnp.roll(li_gain.reshape(2, 8, 2, 128)[:, :, k], (-h, -z), axis=(0, 1))
    gain = jnp.transpose(gain, (1, 0, 2)).reshape(8, 256)

    (parts,) = call(
        branch_body,
        [((4, 512, 256), BF)],
        [g00, g01, across, across_core, *out_blocks],
        scratch=[pltpu.VMEM((1024, 1024), BF)],
        after=[li_near[1], li_near[-1], li_away[1], li_away[-1]],
    )
    turn = jnp.stack([z + 2 * x, l, k]).astype(jnp.int32)
    residual = []
    for dk in range(2):
        part = pl.pallas_call(
            slice_body,
            out_shape=jax.ShapeDtypeStruct((256, 256), BF),
            grid_spec=pltpu.PrefetchScalarGridSpec(
                num_scalar_prefetch=1,
                grid=(2,),
                in_specs=[
                    pl.BlockSpec(
                        (256, 128),
                        lambda n, t, dk=dk: (0, t[1] * 16 + ((t[0] + n) & 7) * 2 + (t[2] ^ dk)),
                    ),
                    pl.BlockSpec(memory_space=pl.ANY),
                ],
                out_specs=pl.BlockSpec((256, 128), lambda n, t: (0, n)),
            ),
        )(turn, stream_in, parts)
        residual.append(part)
    residual[1] = turned(residual[1], "core", 1)
    parts = lax.all_to_all(parts, "xx", 0, 0, tiled=True)
    (stream,) = call(
        stream_body,
        [((8, 512, 256), BF)],
        [parts, *residual],
        after=[blocks[n] for blocks in (li_near, li_away) for n in (2, -2)],
    )
    acts = lax.all_to_all(stream, CHAN, 0, 0, tiled=True)
    own, send, rest = call(
        proj_body,
        [((256, 1664), F32), ((256, 1024), BF), ((256, 896), BF)],
        [place, acts, gain, *li_near, *li_away],
        scratch=[pltpu.VMEM((256, 2048), BF), pltpu.VMEM((2048, 1536), BF)],
        smem=(0,),
        vmem=26,
    )
    li, tail, stream_out = call(
        functools.partial(normed_body, float(width)),
        [((3, 256, 512), BF), ((48, 512), BF), ((256, 512), BF)],
        [place, own, turned(send, "core", 1), turned(rest, "core", 1), acts],
        smem=(0,),
    )
    gate, vals, state = call(
        states_body,
        [((256, 512), F32), ((256, 512), F32), ((16, 512), F32)],
        [li, shifted(tail, SEQ, 1), li_short, li_rate],
    )

    span = float(li.shape[1])
    chips, first = call(
        functools.partial(chip_body, span),
        [((16, 16, 512), BF), ((16, 512), F32)],
        [place, state, turned(state, "core", 1), li_rate],
        smem=(0,),
    )
    chips = lax.all_to_all(chips, CHIPS, 0, 0, tiled=True)
    (base,) = call(
        echo_body,
        [((256, 512), F32)],
        [gate, vals, li_res, li_rate, li_skip.reshape(1, 512)],
        after=[first],
    )
    (li_output,) = call(
        functools.partial(output_body, span),
        [((512, 256), BF)],
        [place, chips, first, li_res, li_rate, gate, base],
        scratch=[pltpu.VMEM((16, 32, 512), F32), pltpu.VMEM((256, 512), F32)],
        smem=(0,),
    )
    return (stream_out, li_output)


def solution(mesh):
    split = Mesh(mesh.devices.reshape(2, 8, 2, 2, 4), ("yh", "z", "core", "yl", "xx"))
    placed = (
        P(SEQ, None),
        P(SEQ, None, CHAN),
        P(None, None, CHAN),
        P(CHAN, None),
        P(CHAN, SEQ),
        P(),
        P(SEQ, None, CHAN),
        P(None, None, CHAN),
        P(None, CHAN),
        P(None, CHAN),
        P(CHAN),
    )
    return jax.shard_map(
        local,
        mesh=split,
        in_specs=placed,
        out_specs=(P(SEQ, CHAN), P(CHAN, SEQ)),
        check_vma=False,
    )
```

```python
import functools

import jax
import jax.numpy as jnp
from jax import lax
from jax.experimental import pallas as pl
from jax.experimental.pallas import tpu as pltpu
from jax.sharding import Mesh
from jax.sharding import PartitionSpec as P

BF = jnp.bfloat16
F32 = jnp.float32
EPSILON = 1e-06
SEQ = ("yh", "z", "core")
CHIPS = ("yh", "z")
CHAN = ("yl", "xx")
GROUP = 16
MIB = 1024 * 1024


def call(body, outs, ins, scratch=(), smem=(), after=(), vmem=32):
    given = len(ins)
    specs = [
        pl.BlockSpec(memory_space=pltpu.SMEM if i in smem else pltpu.VMEM) for i in range(given)
    ]
    specs = specs + [pl.BlockSpec(memory_space=pl.ANY)] * len(after)

    def kernel(*refs):
        body(*refs[:given], *refs[given + len(after) :])

    return pl.pallas_call(
        kernel,
        out_shape=[jax.ShapeDtypeStruct(s, d) for s, d in outs],
        in_specs=specs,
        out_specs=[pl.BlockSpec(memory_space=pltpu.VMEM)] * len(outs),
        scratch_shapes=list(scratch),
        compiler_params=pltpu.CompilerParams(vmem_limit_bytes=vmem * MIB),
    )(*ins, *after)


def shifted(block, axis, distance):
    n = lax.axis_size(axis)
    return lax.ppermute(block, axis, [(i - distance, i) for i in range(distance, n)])


def turned(block, axis, distance):
    n = lax.axis_size(axis)
    return lax.ppermute(block, axis, [(i, (i + distance) % n) for i in range(n)])


def ring(block, axis, way=1):
    n = lax.axis_size(axis)
    out = [None] * n
    out[0] = block
    up = down = block
    for i in range(1, n // 2 + 1):
        if i < n - i or way > 0:
            up = turned(up, axis, 1)
            out[n - i] = up
        if i < n - i or way < 0:
            down = turned(down, axis, -1)
            out[i] = down
    return out


def short3(ext, w):
    return w[0:1] * ext + w[1:2] * pltpu.roll(ext, 1, 0) + w[2:3] * pltpu.roll(ext, 2, 0)


def mr_body(proj, halo, short, rows, gated, vals):
    t = proj.shape[1]
    k = jnp.concatenate([halo[0:144].astype(F32), proj[1].astype(F32)], axis=0)
    v = jnp.concatenate([halo[144:288].astype(F32), proj[2].astype(F32)], axis=0)
    km = short3(k, short[1])
    vm = short3(v, short[2])
    vals[...] = (km * vm)[16:].astype(BF)
    q = jnp.concatenate([halo[288:304].astype(F32), proj[0].astype(F32)], axis=0)
    qm = short3(q, short[0])[16:]
    lane_group = lax.broadcasted_iota(jnp.int32, (128, 128), 1) // GROUP
    for tile in range(proj.shape[2] // 128):
        cols = slice(tile * 128, tile * 128 + 128)
        window = jnp.concatenate(
            [vals[b * 128 : b * 128 + 256, cols] for b in range(t // 128)], axis=1
        )
        acc = [jnp.zeros((128, 128), F32) for _ in range(t // 128)]
        for g in range(8):
            row = rows[tile * 8 + g : tile * 8 + g + 1, :]
            band = pltpu.roll(
                jnp.broadcast_to(row, (128, 256)), 0, 1, stride=1, stride_axis=0
            ).astype(BF)
            got = jnp.dot(band, window, preferred_element_type=F32)
            for b in range(t // 128):
                acc[b] = jnp.where(lane_group == g, got[:, b * 128 : b * 128 + 128], acc[b])
        for b in range(t // 128):
            r = slice(b * 128, b * 128 + 128)
            gated[r, cols] = (qm[r, cols] * acc[b]).astype(BF)


def branch_body(*refs):
    parts, weights = refs[:4], refs[4:12]
    out, ws = refs[12:]
    for j in range(8):
        ws[:, j * 128 : j * 128 + 128] = weights[j][...]
    for n in range(2):
        got = jnp.dot(parts[n][...], ws[:512, :], preferred_element_type=F32)
        got = got + jnp.dot(parts[2 + n][...], ws[512:, :], preferred_element_type=F32)
        for j in range(4):
            out[j, n * 256 : n * 256 + 256, :] = got[:, j * 256 : j * 256 + 256].astype(BF)


def slice_body(place, stream, after, out):
    out[...] = stream[...]


def stream_body(recv, own, core, out):
    for n, rows in enumerate((own, core)):
        r = slice(n * 256, n * 256 + 256)
        total = rows[...].astype(F32)
        for j in range(recv.shape[0]):
            total = total + recv[j, r, :].astype(F32)
        total = total.astype(BF)
        for j in range(out.shape[0]):
            out[j, r, :] = total


def proj_body(*refs):
    place, acts, gain = refs[:3]
    near, away = refs[3:11], refs[11:19]
    own, send, rest, a_s, w_s = refs[19:]
    for j in range(8):
        for p in range(3):
            cols = slice(p * 512, p * 512 + 512)
            w_s[j * 256 : j * 256 + 128, cols] = near[j][p]
            w_s[j * 256 + 128 : j * 256 + 256, cols] = away[j][p]
    lane = lax.broadcasted_iota(jnp.int32, (256, 128), 1)
    for dk in (1, 0):
        squares = jnp.zeros((256, 128), F32)
        for j in range(8):
            for side in range(2):
                half = slice((j % 2) * 128, (j % 2) * 128 + 128)
                a = acts[
                    (place[0] ^ side) * 4 + j // 2, dk * 256 : dk * 256 + 256, half
                ].astype(F32)
                squares = squares + a * a
                scale = gain[j : j + 1, side * 128 : side * 128 + 128]
                cols = slice(j * 256 + side * 128, j * 256 + side * 128 + 128)
                a_s[:, cols] = (a * scale).astype(BF)
        total = jnp.sum(squares, axis=1, keepdims=True)
        for p in range(3):
            cols = slice(p * 512, p * 512 + 512)
            got = jnp.dot(a_s[...], w_s[:, cols], preferred_element_type=F32)
            if dk == 0:
                own[:, cols] = got
            elif p < 2:
                send[:, cols] = got.astype(BF)
            else:
                rest[:, :512] = got.astype(BF)
        if dk == 0:
            own[:, 1536:] = jnp.where(lane == 0, total, 0.0)
        else:
            rest[:, 512:640] = in_two(total, lane)
    for q in range(2):
        half = pl.multiple_of((place[2 + q] & 1) * 128, 128)
        block = place[5] * 4 + (place[2 + q] >> 1)
        rest[:, 640 + q * 128 : 768 + q * 128] = acts[block, 256:, pl.ds(half, 128)]


def assemble(place, acts, rest, out):
    for q in range(2):
        half = pl.multiple_of((place[2 + q] & 1) * 128, 128)
        block = place[5] * 4 + (place[2 + q] >> 1)
        mine = pl.multiple_of(q * 256 + place[1] * 128, 128)
        theirs = pl.multiple_of(q * 256 + 128 - place[1] * 128, 128)
        out[:, pl.ds(mine, 128)] = acts[block, :256, pl.ds(half, 128)]
        out[:, pl.ds(theirs, 128)] = rest[:, 640 + q * 128 : 768 + q * 128]


def in_two(total, lane):
    high = total.astype(BF).astype(F32)
    return jnp.where(lane == 0, high, jnp.where(lane == 1, total - high, 0.0)).astype(BF)


def normed_body(width, place, own, recv, rest, acts, out, tail, stream):
    sums = own[:, 1536:] + rest[:, 512:640].astype(F32)
    scale = lax.rsqrt(jnp.sum(sums, axis=1, keepdims=True) / width + EPSILON)
    for p in range(3):
        c = slice(p * 512, p * 512 + 512)
        other = recv[:, c] if p < 2 else rest[:, :512]
        got = ((own[:, c] + other.astype(F32)) * scale).astype(BF)
        out[p] = got
        tail[p * 16 : p * 16 + 16, :] = got[240:, :]
    assemble(place, acts, rest, stream)


def states_body(li, halo, short, rate, gate, vals, state):
    mixed = []
    for p in range(3):
        ext = jnp.concatenate(
            [halo[p * 16 : p * 16 + 16].astype(F32), li[p].astype(F32)], axis=0
        )
        mixed.append(short3(ext, short[p])[16:])
    gate[...] = mixed[0]
    vals[...] = (mixed[1] * mixed[2]).astype(BF).astype(F32)
    decay = jnp.exp(-rate[...])

    def eight(i, s):
        v = vals[pl.ds(pl.multiple_of(i * 8, 8), 8), :]
        for r in range(8):
            s = decay * s + v[r : r + 1, :]
        return s

    state[...] = lax.fori_loop(0, 32, eight, jnp.zeros_like(decay))


def chip_body(span, place, state, other, rate, out, first):
    low = place[1] == 0
    early = jnp.where(low, state[...], other[...])
    late = jnp.where(low, other[...], state[...])
    first[...] = early
    chip = (late + jnp.exp(-rate[...] * span) * early).astype(BF)
    for j in range(out.shape[0]):
        out[j] = chip


def echo_body(gate, vals, res, rate, skip, base):
    decay = jnp.exp(-rate[...])
    residues = res[...]

    def eight(i, s):
        rows = pl.ds(pl.multiple_of(i * 8, 8), 8)
        v = vals[rows, :]
        got = []
        for r in range(8):
            s = decay * s + v[r : r + 1, :]
            got.append(jnp.sum(residues * s, axis=0, keepdims=True))
        base[rows, :] = gate[rows, :] * (jnp.concatenate(got, axis=0) + skip[...] * v)
        return s

    lax.fori_loop(0, 32, eight, jnp.zeros_like(decay))


def output_body(span, place, chips, first, res, rate, gate, base, out, fade, ys):
    rates = rate[...]
    over = jnp.exp(-rates * span)
    twice = jnp.exp(-rates * (2.0 * span))
    entering = jnp.zeros_like(rates)
    for j in range(chips.shape[0]):
        entering = jnp.where(j < place[4], twice * entering + chips[j].astype(F32), entering)
    entering = jnp.where(place[1] == 0, entering, first[...] + over * entering)
    weights = res[...] * entering
    modes, tile = fade.shape[:2]
    step = (lax.broadcasted_iota(jnp.int32, fade.shape[1:], 0) + 1).astype(F32)
    for r in range(modes):
        fade[r] = jnp.exp(-rates[r : r + 1, :] * step)
    past = jnp.exp(-rates * float(tile))
    for b in range(ys.shape[0] // tile):
        rows = slice(b * tile, b * tile + tile)
        total = jnp.zeros(fade.shape[1:], F32)
        for r in range(modes):
            total = total + weights[r : r + 1, :] * fade[r]
        ys[rows, :] = base[rows, :] + gate[rows, :] * total
        weights = weights * past
    out[...] = ys[...].T.astype(BF)


def local(
    stream_in,
    mr_proj,
    mr_short,
    mr_filter,
    mr_out,
    li_gain,
    li_in,
    li_short,
    li_res,
    li_rate,
    li_skip,
):
    h, z, k = (lax.axis_index(a) for a in SEQ)
    l, x = (lax.axis_index(a) for a in CHAN)
    width = stream_in.shape[1]
    place = jnp.stack([h, k, (2 * x - z) % 8, (2 * x + 1 - z) % 8, h * 8 + z, l]).astype(jnp.int32)

    proj = jnp.transpose(mr_proj, (1, 0, 2))
    halo = shifted(
        jnp.concatenate([proj[1, -144:], proj[2, -144:], proj[0, -16:]], axis=0), SEQ, 1
    )
    here = mr_out
    first = lax.ppermute(here, ("yh", "yl"), [(1, 0), (2, 3), (0, 2), (3, 1)])
    second = lax.ppermute(here, ("yh", "yl"), [(1, 2), (2, 1)])
    pair = [jnp.where(h == l, here, first), jnp.where(h == l, first, second)]
    out_blocks = ring(jnp.concatenate(pair, axis=0), "z")
    taps = mr_filter.shape[1]
    rows = jnp.pad(mr_filter[:, ::-1], ((0, 0), (1, 255 - taps)))
    (g00,) = call(
        mr_body,
        [((256, 512), BF)],
        [proj, halo, mr_short, rows],
        scratch=[pltpu.VMEM((384, 512), BF)],
        after=[out_blocks[1], out_blocks[-1]],
    )
    across = turned(g00, "yl", 1)
    g01, across_core = turned(g00, "core", 1), turned(across, "core", 1)
    li_own = jnp.transpose(li_in, (1, 0, 2))
    li_side = turned(li_own, "yh", 1)
    li_near, li_away = ring(li_own, "z"), ring(li_side, "z", -1)
    gain = jnp.roll(li_gain.reshape(2, 8, 2, 128)[:, :, k], (-h, -z), axis=(0, 1))
    gain = jnp.transpose(gain, (1, 0, 2)).reshape(8, 256)

    def ordered(value, *hops):
        picks = [(blocks, n) for blocks in (li_near, li_away) for n in hops]
        value, *come = lax.optimization_barrier((value, *[blocks[n] for blocks, n in picks]))
        for (blocks, n), block in zip(picks, come):
            blocks[n] = block
        return value

    across_core = ordered(across_core, 1, -1)
    (parts,) = call(
        branch_body,
        [((4, 512, 256), BF)],
        [g00, g01, across, across_core, *out_blocks],
        scratch=[pltpu.VMEM((1024, 1024), BF)],
    )
    turn = jnp.stack([z + 2 * x, l, k]).astype(jnp.int32)
    residual = []
    for dk in range(2):
        part = pl.pallas_call(
            slice_body,
            out_shape=jax.ShapeDtypeStruct((256, 256), BF),
            grid_spec=pltpu.PrefetchScalarGridSpec(
                num_scalar_prefetch=1,
                grid=(2,),
                in_specs=[
                    pl.BlockSpec(
                        (256, 128),
                        lambda n, t, dk=dk: (0, t[1] * 16 + ((t[0] + n) & 7) * 2 + (t[2] ^ dk)),
                    ),
                    pl.BlockSpec(memory_space=pl.ANY),
                ],
                out_specs=pl.BlockSpec((256, 128), lambda n, t: (0, n)),
            ),
        )(turn, stream_in, parts)
        residual.append(part)
    residual[1] = turned(residual[1], "core", 1)
    parts = ordered(lax.all_to_all(parts, "xx", 0, 0, tiled=True), 2, -2)
    (stream,) = call(
        stream_body,
        [((8, 512, 256), BF)],
        [parts, *residual],
    )
    acts = lax.all_to_all(stream, CHAN, 0, 0, tiled=True)
    own, send, rest = call(
        proj_body,
        [((256, 1664), F32), ((256, 1024), BF), ((256, 896), BF)],
        [place, acts, gain, *li_near, *li_away],
        scratch=[pltpu.VMEM((256, 2048), BF), pltpu.VMEM((2048, 1536), BF)],
        smem=(0,),
        vmem=26,
    )
    li, tail, stream_out = call(
        functools.partial(normed_body, float(width)),
        [((3, 256, 512), BF), ((48, 512), BF), ((256, 512), BF)],
        [place, own, turned(send, "core", 1), turned(rest, "core", 1), acts],
        smem=(0,),
    )
    gate, vals, state = call(
        states_body,
        [((256, 512), F32), ((256, 512), F32), ((16, 512), F32)],
        [li, shifted(tail, SEQ, 1), li_short, li_rate],
    )

    span = float(li.shape[1])
    chips, first = call(
        functools.partial(chip_body, span),
        [((16, 16, 512), BF), ((16, 512), F32)],
        [place, state, turned(state, "core", 1), li_rate],
        smem=(0,),
    )
    chips = lax.all_to_all(chips, CHIPS, 0, 0, tiled=True)
    (base,) = call(
        echo_body,
        [((256, 512), F32)],
        [gate, vals, li_res, li_rate, li_skip.reshape(1, 512)],
        after=[first],
    )
    (li_output,) = call(
        functools.partial(output_body, span),
        [((512, 256), BF)],
        [place, chips, first, li_res, li_rate, gate, base],
        scratch=[pltpu.VMEM((16, 32, 512), F32), pltpu.VMEM((256, 512), F32)],
        smem=(0,),
    )
    return (stream_out, li_output)


def solution(mesh):
    split = Mesh(mesh.devices.reshape(2, 8, 2, 2, 4), ("yh", "z", "core", "yl", "xx"))
    placed = (
        P(SEQ, None),
        P(SEQ, None, CHAN),
        P(None, None, CHAN),
        P(CHAN, None),
        P(CHAN, SEQ),
        P(),
        P(SEQ, None, CHAN),
        P(None, None, CHAN),
        P(None, CHAN),
        P(None, CHAN),
        P(CHAN),
    )
    return jax.shard_map(
        local,
        mesh=split,
        in_specs=placed,
        out_specs=(P(SEQ, CHAN), P(CHAN, SEQ)),
        check_vma=False,
    )
```

```python
import functools

import jax
import jax.numpy as jnp
from jax import lax
from jax.experimental import pallas as pl
from jax.experimental.pallas import tpu as pltpu
from jax.sharding import Mesh
from jax.sharding import PartitionSpec as P

BF = jnp.bfloat16
F32 = jnp.float32
EPSILON = 1e-06
SEQ = ("yh", "z", "core")
CHIPS = ("yh", "z")
CHAN = ("yl", "xx")
GROUP = 16
MIB = 1024 * 1024


def call(body, outs, ins, scratch=(), smem=(), after=(), vmem=32):
    given = len(ins)
    specs = [
        pl.BlockSpec(memory_space=pltpu.SMEM if i in smem else pltpu.VMEM) for i in range(given)
    ]
    specs = specs + [pl.BlockSpec(memory_space=pl.ANY)] * len(after)

    def kernel(*refs):
        body(*refs[:given], *refs[given + len(after) :])

    return pl.pallas_call(
        kernel,
        out_shape=[jax.ShapeDtypeStruct(s, d) for s, d in outs],
        in_specs=specs,
        out_specs=[pl.BlockSpec(memory_space=pltpu.VMEM)] * len(outs),
        scratch_shapes=list(scratch),
        compiler_params=pltpu.CompilerParams(vmem_limit_bytes=vmem * MIB),
    )(*ins, *after)


def shifted(block, axis, distance):
    n = lax.axis_size(axis)
    return lax.ppermute(block, axis, [(i - distance, i) for i in range(distance, n)])


def turned(block, axis, distance):
    n = lax.axis_size(axis)
    return lax.ppermute(block, axis, [(i, (i + distance) % n) for i in range(n)])


def ring(block, axis, way=1):
    n = lax.axis_size(axis)
    out = [None] * n
    out[0] = block
    up = down = block
    for i in range(1, n // 2 + 1):
        if i < n - i or way > 0:
            up = turned(up, axis, 1)
            out[n - i] = up
        if i < n - i or way < 0:
            down = turned(down, axis, -1)
            out[i] = down
    return out


def short3(ext, w):
    return w[0:1] * ext + w[1:2] * pltpu.roll(ext, 1, 0) + w[2:3] * pltpu.roll(ext, 2, 0)


def mr_body(proj, halo, short, rows, gated, vals):
    t = proj.shape[1]
    k = jnp.concatenate([halo[0:144].astype(F32), proj[1].astype(F32)], axis=0)
    v = jnp.concatenate([halo[144:288].astype(F32), proj[2].astype(F32)], axis=0)
    km = short3(k, short[1])
    vm = short3(v, short[2])
    vals[...] = (km * vm)[16:].astype(BF)
    q = jnp.concatenate([halo[288:304].astype(F32), proj[0].astype(F32)], axis=0)
    qm = short3(q, short[0])[16:]
    lane_group = lax.broadcasted_iota(jnp.int32, (128, 128), 1) // GROUP
    for tile in range(proj.shape[2] // 128):
        cols = slice(tile * 128, tile * 128 + 128)
        window = jnp.concatenate(
            [vals[b * 128 : b * 128 + 256, cols] for b in range(t // 128)], axis=1
        )
        acc = [jnp.zeros((128, 128), F32) for _ in range(t // 128)]
        for g in range(8):
            row = rows[tile * 8 + g : tile * 8 + g + 1, :]
            band = pltpu.roll(
                jnp.broadcast_to(row, (128, 256)), 0, 1, stride=1, stride_axis=0
            ).astype(BF)
            got = jnp.dot(band, window, preferred_element_type=F32)
            for b in range(t // 128):
                acc[b] = jnp.where(lane_group == g, got[:, b * 128 : b * 128 + 128], acc[b])
        for b in range(t // 128):
            r = slice(b * 128, b * 128 + 128)
            gated[r, cols] = (qm[r, cols] * acc[b]).astype(BF)


def branch_body(*refs):
    parts, weights = refs[:4], refs[4:12]
    out, ws = refs[12:]
    for j in range(8):
        ws[:, j * 128 : j * 128 + 128] = weights[j][...]
    for n in range(2):
        got = jnp.dot(parts[n][...], ws[:512, :], preferred_element_type=F32)
        got = got + jnp.dot(parts[2 + n][...], ws[512:, :], preferred_element_type=F32)
        for j in range(4):
            out[j, n * 256 : n * 256 + 256, :] = got[:, j * 256 : j * 256 + 256].astype(BF)


def slice_body(place, stream, after, out):
    out[...] = stream[...]


def stream_body(recv, own, core, out):
    for n, rows in enumerate((own, core)):
        r = slice(n * 256, n * 256 + 256)
        total = rows[...].astype(F32)
        for j in range(recv.shape[0]):
            total = total + recv[j, r, :].astype(F32)
        total = total.astype(BF)
        for j in range(out.shape[0]):
            out[j, r, :] = total


def proj_body(*refs):
    place, acts, gain = refs[:3]
    near, away = refs[3:11], refs[11:19]
    own, send, rest, a_s, w_s = refs[19:]
    for j in range(8):
        for p in range(3):
            cols = slice(p * 512, p * 512 + 512)
            w_s[j * 256 : j * 256 + 128, cols] = near[j][p]
            w_s[j * 256 + 128 : j * 256 + 256, cols] = away[j][p]
    lane = lax.broadcasted_iota(jnp.int32, (256, 128), 1)
    squares = jnp.zeros((512, 128), F32)
    for j in range(8):
        for side in range(2):
            half = slice((j % 2) * 128, (j % 2) * 128 + 128)
            a = acts[(place[0] ^ side) * 4 + j // 2, :, half].astype(F32)
            squares = squares + a * a
            scale = gain[j : j + 1, side * 128 : side * 128 + 128]
            cols = slice(j * 256 + side * 128, j * 256 + side * 128 + 128)
            a_s[:, cols] = (a * scale).astype(BF)
    total = jnp.sum(squares, axis=1, keepdims=True)
    own[:, 1536:] = jnp.where(lane == 0, total[:256], 0.0)
    rest[:, 512:640] = in_two(total[256:], lane)
    for p in range(3):
        cols = slice(p * 512, p * 512 + 512)
        got = jnp.dot(a_s[...], w_s[:, cols], preferred_element_type=F32)
        own[:, cols] = got[:256]
        if p < 2:
            send[:, cols] = got[256:].astype(BF)
        else:
            rest[:, :512] = got[256:].astype(BF)
    for q in range(2):
        half = pl.multiple_of((place[2 + q] & 1) * 128, 128)
        block = place[5] * 4 + (place[2 + q] >> 1)
        rest[:, 640 + q * 128 : 768 + q * 128] = acts[block, 256:, pl.ds(half, 128)]


def assemble(place, acts, rest, out):
    for q in range(2):
        half = pl.multiple_of((place[2 + q] & 1) * 128, 128)
        block = place[5] * 4 + (place[2 + q] >> 1)
        mine = pl.multiple_of(q * 256 + place[1] * 128, 128)
        theirs = pl.multiple_of(q * 256 + 128 - place[1] * 128, 128)
        out[:, pl.ds(mine, 128)] = acts[block, :256, pl.ds(half, 128)]
        out[:, pl.ds(theirs, 128)] = rest[:, 640 + q * 128 : 768 + q * 128]


def in_two(total, lane):
    high = total.astype(BF).astype(F32)
    return jnp.where(lane == 0, high, jnp.where(lane == 1, total - high, 0.0)).astype(BF)


def normed_body(width, place, own, recv, rest, acts, out, tail, stream):
    sums = own[:, 1536:] + rest[:, 512:640].astype(F32)
    scale = lax.rsqrt(jnp.sum(sums, axis=1, keepdims=True) / width + EPSILON)
    for p in range(3):
        c = slice(p * 512, p * 512 + 512)
        other = recv[:, c] if p < 2 else rest[:, :512]
        got = ((own[:, c] + other.astype(F32)) * scale).astype(BF)
        out[p] = got
        tail[p * 16 : p * 16 + 16, :] = got[240:, :]
    assemble(place, acts, rest, stream)


def states_body(li, halo, short, rate, gate, vals, state):
    mixed = []
    for p in range(3):
        ext = jnp.concatenate(
            [halo[p * 16 : p * 16 + 16].astype(F32), li[p].astype(F32)], axis=0
        )
        mixed.append(short3(ext, short[p])[16:])
    gate[...] = mixed[0]
    vals[...] = (mixed[1] * mixed[2]).astype(BF).astype(F32)
    decay = jnp.exp(-rate[...])

    def eight(i, s):
        v = vals[pl.ds(pl.multiple_of(i * 8, 8), 8), :]
        for r in range(8):
            s = decay * s + v[r : r + 1, :]
        return s

    state[...] = lax.fori_loop(0, 32, eight, jnp.zeros_like(decay))


def chip_body(span, place, state, other, rate, out, first):
    low = place[1] == 0
    early = jnp.where(low, state[...], other[...])
    late = jnp.where(low, other[...], state[...])
    first[...] = early
    chip = (late + jnp.exp(-rate[...] * span) * early).astype(BF)
    for j in range(out.shape[0]):
        out[j] = chip


def echo_body(gate, vals, res, rate, skip, base):
    decay = jnp.exp(-rate[...])
    residues = res[...]

    def eight(i, s):
        rows = pl.ds(pl.multiple_of(i * 8, 8), 8)
        v = vals[rows, :]
        got = []
        for r in range(8):
            s = decay * s + v[r : r + 1, :]
            got.append(jnp.sum(residues * s, axis=0, keepdims=True))
        base[rows, :] = gate[rows, :] * (jnp.concatenate(got, axis=0) + skip[...] * v)
        return s

    lax.fori_loop(0, 32, eight, jnp.zeros_like(decay))


def output_body(span, place, chips, first, res, rate, gate, base, out, fade, ys):
    rates = rate[...]
    over = jnp.exp(-rates * span)
    twice = jnp.exp(-rates * (2.0 * span))
    entering = jnp.zeros_like(rates)
    for j in range(chips.shape[0]):
        entering = jnp.where(j < place[4], twice * entering + chips[j].astype(F32), entering)
    entering = jnp.where(place[1] == 0, entering, first[...] + over * entering)
    weights = res[...] * entering
    modes, tile = fade.shape[:2]
    step = (lax.broadcasted_iota(jnp.int32, fade.shape[1:], 0) + 1).astype(F32)
    for r in range(modes):
        fade[r] = jnp.exp(-rates[r : r + 1, :] * step)
    past = jnp.exp(-rates * float(tile))
    for b in range(ys.shape[0] // tile):
        rows = slice(b * tile, b * tile + tile)
        total = jnp.zeros(fade.shape[1:], F32)
        for r in range(modes):
            total = total + weights[r : r + 1, :] * fade[r]
        ys[rows, :] = base[rows, :] + gate[rows, :] * total
        weights = weights * past
    out[...] = ys[...].T.astype(BF)


def local(
    stream_in,
    mr_proj,
    mr_short,
    mr_filter,
    mr_out,
    li_gain,
    li_in,
    li_short,
    li_res,
    li_rate,
    li_skip,
):
    h, z, k = (lax.axis_index(a) for a in SEQ)
    l, x = (lax.axis_index(a) for a in CHAN)
    width = stream_in.shape[1]
    place = jnp.stack([h, k, (2 * x - z) % 8, (2 * x + 1 - z) % 8, h * 8 + z, l]).astype(jnp.int32)

    proj = jnp.transpose(mr_proj, (1, 0, 2))
    halo = shifted(
        jnp.concatenate([proj[1, -144:], proj[2, -144:], proj[0, -16:]], axis=0), SEQ, 1
    )
    here = mr_out
    first = lax.ppermute(here, ("yh", "yl"), [(1, 0), (2, 3), (0, 2), (3, 1)])
    second = lax.ppermute(here, ("yh", "yl"), [(1, 2), (2, 1)])
    pair = [jnp.where(h == l, here, first), jnp.where(h == l, first, second)]
    out_blocks = ring(jnp.concatenate(pair, axis=0), "z")
    taps = mr_filter.shape[1]
    rows = jnp.pad(mr_filter[:, ::-1], ((0, 0), (1, 255 - taps)))
    (g00,) = call(
        mr_body,
        [((256, 512), BF)],
        [proj, halo, mr_short, rows],
        scratch=[pltpu.VMEM((384, 512), BF)],
        after=[out_blocks[1], out_blocks[-1]],
    )
    across = turned(g00, "yl", 1)
    g01, across_core = turned(g00, "core", 1), turned(across, "core", 1)
    li_own = jnp.transpose(li_in, (1, 0, 2))
    li_side = turned(li_own, "yh", 1)
    li_near, li_away = ring(li_own, "z"), ring(li_side, "z", -1)
    gain = jnp.roll(li_gain.reshape(2, 8, 2, 128)[:, :, k], (-h, -z), axis=(0, 1))
    gain = jnp.transpose(gain, (1, 0, 2)).reshape(8, 256)

    def ordered(value, *hops):
        picks = [(blocks, n) for blocks in (li_near, li_away) for n in hops]
        value, *come = lax.optimization_barrier((value, *[blocks[n] for blocks, n in picks]))
        for (blocks, n), block in zip(picks, come):
            blocks[n] = block
        return value

    across_core = ordered(across_core, 1, -1)
    (parts,) = call(
        branch_body,
        [((4, 512, 256), BF)],
        [g00, g01, across, across_core, *out_blocks],
        scratch=[pltpu.VMEM((1024, 1024), BF)],
    )
    turn = jnp.stack([z + 2 * x, l, k]).astype(jnp.int32)
    residual = []
    for dk in range(2):
        part = pl.pallas_call(
            slice_body,
            out_shape=jax.ShapeDtypeStruct((256, 256), BF),
            grid_spec=pltpu.PrefetchScalarGridSpec(
                num_scalar_prefetch=1,
                grid=(2,),
                in_specs=[
                    pl.BlockSpec(
                        (256, 128),
                        lambda n, t, dk=dk: (0, t[1] * 16 + ((t[0] + n) & 7) * 2 + (t[2] ^ dk)),
                    ),
                    pl.BlockSpec(memory_space=pl.ANY),
                ],
                out_specs=pl.BlockSpec((256, 128), lambda n, t: (0, n)),
            ),
        )(turn, stream_in, parts)
        residual.append(part)
    residual[1] = turned(residual[1], "core", 1)
    parts = ordered(lax.all_to_all(parts, "xx", 0, 0, tiled=True), 2, -2)
    (stream,) = call(
        stream_body,
        [((8, 512, 256), BF)],
        [parts, *residual],
    )
    acts = lax.all_to_all(stream, CHAN, 0, 0, tiled=True)
    own, send, rest = call(
        proj_body,
        [((256, 1664), F32), ((256, 1024), BF), ((256, 896), BF)],
        [place, acts, gain, *li_near, *li_away],
        scratch=[pltpu.VMEM((512, 2048), BF), pltpu.VMEM((2048, 1536), BF)],
        smem=(0,),
        vmem=26,
    )
    li, tail, stream_out = call(
        functools.partial(normed_body, float(width)),
        [((3, 256, 512), BF), ((48, 512), BF), ((256, 512), BF)],
        [place, own, turned(send, "core", 1), turned(rest, "core", 1), acts],
        smem=(0,),
    )
    gate, vals, state = call(
        states_body,
        [((256, 512), F32), ((256, 512), F32), ((16, 512), F32)],
        [li, shifted(tail, SEQ, 1), li_short, li_rate],
    )

    span = float(li.shape[1])
    chips, first = call(
        functools.partial(chip_body, span),
        [((16, 16, 512), BF), ((16, 512), F32)],
        [place, state, turned(state, "core", 1), li_rate],
        smem=(0,),
    )
    chips = lax.all_to_all(chips, CHIPS, 0, 0, tiled=True)
    (base,) = call(
        echo_body,
        [((256, 512), F32)],
        [gate, vals, li_res, li_rate, li_skip.reshape(1, 512)],
        after=[first],
    )
    (li_output,) = call(
        functools.partial(output_body, span),
        [((512, 256), BF)],
        [place, chips, first, li_res, li_rate, gate, base],
        scratch=[pltpu.VMEM((16, 32, 512), F32), pltpu.VMEM((256, 512), F32)],
        smem=(0,),
    )
    return (stream_out, li_output)


def solution(mesh):
    split = Mesh(mesh.devices.reshape(2, 8, 2, 2, 4), ("yh", "z", "core", "yl", "xx"))
    placed = (
        P(SEQ, None),
        P(SEQ, None, CHAN),
        P(None, None, CHAN),
        P(CHAN, None),
        P(CHAN, SEQ),
        P(),
        P(SEQ, None, CHAN),
        P(None, None, CHAN),
        P(None, CHAN),
        P(None, CHAN),
        P(CHAN),
    )
    return jax.shard_map(
        local,
        mesh=split,
        in_specs=placed,
        out_specs=(P(SEQ, CHAN), P(CHAN, SEQ)),
        check_vma=False,
    )
```
